32 devices in a mesh: freq: 8 (over z, y), half: 4 (over x, core).
Axes of the slice: x: 2, y: 2, z: 4, core: 2. Of those that a mesh axis runs over, the one named last changes fastest.
Arguments:
- voltages: bfloat16 [4, 32, 2, 512, 1024], P('half', 'freq'), may hold values from -127 to 127
- scale_exps: int32 [4, 32, 1024], P('half', 'freq'), may hold values from 0 to 3
Outputs:
- visibilities: bfloat16 [1024, 512, 2, 1024], P('half', 'freq')
The draws below stay inside these ranges and needn't reach their ends.
All inputs are finite; a program needn't handle non-finite values.
Results may differ from the reference program's by a relative error of at most 0.0072.
Values may be sent and summed in bfloat16 or wider, within the bound.
No kernel may reach another device: no remote copies, remote signals or barrier semaphores. Data moves between devices by JAX's collectives and lax.ppermute only.
A program may use at most 384 MiB of HBM per device.

```python
import math
import jax
import jax.numpy as jnp
from jax import lax

CHANNELS = 512
INPUTS = 1024
HALVES = 4
BLOCKS_HALF = 32


def with_ends(array, own_key, low, top_value):
    spot = [jax.random.randint(jax.random.fold_in(own_key, axis), (), 0, length) for axis, length in enumerate(array.shape)]
    longest = array.shape.index(max(array.shape))
    next_to = spot[:longest] + [(spot[longest] + 1) % array.shape[longest]] + spot[longest + 1:]
    return array.at[tuple(spot)].set(low).at[tuple(next_to)].set(top_value)


def level_of(stream_key, dims, shards, smallest, top_value):
    level = 1.0
    for axis_at, blocks in shards:
        draws = jax.random.uniform(jax.random.fold_in(jax.random.fold_in(stream_key, 6), axis_at), (blocks,), jnp.float32, smallest / len(shards), top_value / len(shards))
        level = level * jnp.repeat(jnp.exp(draws), dims[axis_at] // blocks).reshape((-1,) + (1,) * (len(dims) - 1 - axis_at))
    return level


def centred(key, extent, scale, limit, pieces=(), kind=jnp.bfloat16):
    entries = jax.random.normal(key, extent, jnp.float32) * scale
    if len(pieces) > 0:
        entries = level_of(key, extent, pieces, -0.22, 0.18) * entries
    return jnp.clip(entries, min=-limit, max=limit).astype(kind)


def setup_inputs(seed: int = 0) -> dict:
    arg_keys = jax.random.split(jax.random.key(seed), 3)
    return {
        "voltages": centred(arg_keys[0], (HALVES, BLOCKS_HALF, 2, CHANNELS, INPUTS), 24.0, 127.0, ((0, 4), (1, 8))),
        "scale_exps": with_ends(jax.random.randint(arg_keys[1], (HALVES, BLOCKS_HALF, INPUTS), 0, 4), jax.random.fold_in(arg_keys[1], 1), 0, 3).astype(jnp.int32),
    }


def make_window(count):
    steps = jnp.arange(4 * count, dtype=jnp.float32) + 0.5
    return jnp.sinc(steps / count - 2.0) * (0.5 - 0.5 * jnp.cos(2.0 * math.pi * steps / (4 * count)))

def dft_table(count):
    index = jnp.arange(count, dtype=jnp.int32)
    angle = 2.0 * math.pi / count * (index[:, None] * index[None, :] % count).astype(jnp.float32)
    cosine = jnp.cos(angle)
    sine = jnp.sin(angle)
    upper = jnp.concatenate([cosine, sine], axis=1)
    lower = jnp.concatenate([-sine, cosine], axis=1)
    return jnp.concatenate([upper, lower], axis=0).astype(jnp.bfloat16)

def channelize(scaled):
    taps = make_window(CHANNELS).reshape(4, CHANNELS)
    padded = jnp.concatenate([jnp.zeros((3,) + scaled.shape[1:], jnp.float32), scaled], axis=0)
    filtered = jnp.zeros(scaled.shape, jnp.float32)
    for q in range(4):
        filtered = filtered + padded[q:q + BLOCKS_HALF] * taps[q][None, None, :, None]
    filtered = filtered.astype(jnp.bfloat16).astype(jnp.float32)
    table = dft_table(CHANNELS).astype(jnp.float32)
    flat = filtered.reshape(BLOCKS_HALF, 2 * CHANNELS, INPUTS)
    spectrum = jnp.einsum('pq,tqi->tpi', table, flat) * (1.0 / (256.0 * math.sqrt(CHANNELS)))
    return spectrum.reshape(BLOCKS_HALF, 2, CHANNELS, INPUTS).astype(jnp.bfloat16)

def reference(voltages, scale_exps):

    def one_half(pair):
        volts, exps = pair
        scaled = volts.astype(jnp.float32) * jnp.exp2(exps.astype(jnp.float32))[:, None, None, :]
        scaled = scaled.astype(jnp.bfloat16).astype(jnp.float32)
        return channelize(scaled)
    spectra = lax.map(one_half, (voltages, scale_exps))
    weight = 1.0 / (HALVES * BLOCKS_HALF)

    def one_channel(channel):
        values = lax.dynamic_index_in_dim(spectra, channel, 3, keepdims=False).astype(jnp.float32)
        swapped = jnp.stack([values[:, :, 1], -values[:, :, 0]], axis=2)
        left = jnp.stack([values, swapped], axis=0)
        part = jnp.einsum('phtkr,htkj->hrpj', left, values) * weight
        part = lax.optimization_barrier(part.astype(jnp.bfloat16)).astype(jnp.float32)
        return lax.optimization_barrier(jnp.sum(part, axis=0))
    result = lax.map(one_channel, jnp.arange(CHANNELS, dtype=jnp.int32))
    return jnp.transpose(result, (1, 0, 2, 3)).astype(jnp.bfloat16)
```

```python
import functools
import math

import jax
import jax.numpy as jnp
from jax import lax
from jax.experimental import pallas as pl
from jax.experimental.pallas import tpu as pltpu
from jax.sharding import PartitionSpec as P

TAPS = 4
CHUNKS = 4
LANES = 128
VMEM = 56 * 1024 * 1024
SMALL = pl.CostEstimate(flops=1000000, bytes_accessed=100000, transcendentals=0)


def make_window(count):
    steps = jnp.arange(TAPS * count, dtype=jnp.float32) + 0.5
    return jnp.sinc(steps / count - 2.0) * (
        0.5 - 0.5 * jnp.cos(2.0 * math.pi * steps / (TAPS * count))
    )


def dft_table(count, groups, chunks):
    per = count // (groups * chunks)
    index = jnp.arange(count, dtype=jnp.int32)
    channel = index.reshape(groups, chunks, per).transpose(1, 0, 2).reshape(count)
    angle = 2.0 * math.pi / count * (channel[:, None] * index[None, :] % count).astype(jnp.float32)
    cosine = jnp.cos(angle).astype(jnp.bfloat16)
    sine = jnp.sin(angle).astype(jnp.bfloat16)
    upper = jnp.concatenate([cosine, sine], axis=1).reshape(chunks, groups, 1, per, 2 * count)
    lower = jnp.concatenate([-sine, cosine], axis=1).reshape(chunks, groups, 1, per, 2 * count)
    return jnp.concatenate([upper, lower], axis=2).reshape(chunks, 2 * count // chunks, 2 * count)


def channelize_kernel(
    norm, odd_ref, own_ref, scale_ref, got_ref, rim_ref, taps_ref, table_ref, *rest
):
    outs, filtered, spread = rest[:-2], rest[-2], rest[-1]
    blocks, _, count, width = own_ref.shape
    times = 2 * blocks
    chunks, chunk_rows, _ = table_ref.shape
    odd = odd_ref[0] == 1

    def filter_rows(step, carry):
        rows = pl.ds(pl.multiple_of(step * 16, 16), 16)
        weights = [taps_ref[q, rows, :] for q in range(TAPS)]
        for part in range(2):
            for lane in range(0, width, LANES):
                lanes = slice(lane, lane + LANES)
                own = [
                    own_ref[b, part, rows, lanes].astype(jnp.float32) * scale_ref[b : b + 1, lanes]
                    for b in range(blocks)
                ]
                got = [got_ref[b, part, rows, lanes].astype(jnp.float32) for b in range(blocks)]
                line = [
                    rim_ref[b, part, rows, lanes].astype(jnp.float32) for b in range(TAPS - 1)
                ]
                line += [jnp.where(odd, g, o) for g, o in zip(got, own)]
                line += [jnp.where(odd, o, g) for g, o in zip(got, own)]
                at = pl.ds(pl.multiple_of(part * count + step * 16, 16), 16)
                for t in range(times):
                    total = weights[0] * line[t]
                    for q in range(1, TAPS):
                        total = total + weights[q] * line[t + q]
                    filtered[t, at, lanes] = total.astype(jnp.bfloat16)
        return carry

    lax.fori_loop(0, count // 16, filter_rows, 0)

    groups = outs[0].shape[0]
    depth = outs[0].shape[2]
    per = chunk_rows // (2 * groups)
    whole_table = table_ref[...].reshape(chunks * chunk_rows, 2 * count)

    def one_time(t, carry):
        spectrum = jnp.dot(whole_table, filtered[t], preferred_element_type=jnp.float32) * norm
        for block in range(chunks * groups):
            for part in range(2):
                first = (block * 2 + part) * per
                for lane in range(width // LANES):
                    spread[
                        lane, pl.ds(block * per * depth + part * times + t, per, stride=depth), :
                    ] = spectrum[first : first + per, lane * LANES : (lane + 1) * LANES]
        return carry

    lax.fori_loop(0, times, one_time, 0)

    for chunk in range(chunks):
        share = chunks // len(outs)
        out = outs[chunk // share]
        skip = chunk % share * per
        for group in range(groups):
            for c in range(per):
                base = ((chunk * groups + group) * per + c) * depth
                for lane in range(width // LANES):
                    out[group, skip + c, :, lane * LANES : (lane + 1) * LANES] = spread[
                        lane, base : base + depth, :
                    ].astype(jnp.bfloat16)


def channelize(odd, own, scale, got, rims, taps, table, groups, norm, offset, split):
    blocks, _, count, inputs = own.shape
    width = got.shape[3]
    tiles = inputs // 2 // width
    skip = offset // width
    chunks = table.shape[0]
    channels = count // groups // split
    depth = 4 * blocks
    out_shape = (groups, channels, depth, width)
    grid_spec = pltpu.PrefetchScalarGridSpec(
        num_scalar_prefetch=1,
        grid=(1,),
        in_specs=[
            pl.BlockSpec((blocks, 2, count, width), lambda i, o: (0, 0, 0, o[0] * tiles + skip)),
            pl.BlockSpec((blocks, width), lambda i, o: (0, o[0] * tiles + skip)),
            pl.BlockSpec((blocks, 2, count, width), lambda i, o: (0, 0, 0, 0)),
            pl.BlockSpec((TAPS - 1, 2, count, width), lambda i, o: (0, 0, 0, 0)),
            pl.BlockSpec((TAPS, count, LANES), lambda i, o: (0, 0, 0)),
            pl.BlockSpec(table.shape, lambda i, o: (0, 0, 0)),
        ],
        out_specs=[
            pl.BlockSpec(out_shape, lambda i, o: (0, 0, 0, 0))
            for _ in range(split)
        ],
        scratch_shapes=[
            pltpu.VMEM((2 * blocks, 2 * count, width), jnp.bfloat16),
            pltpu.VMEM((width // LANES, count * depth, LANES), jnp.float32),
        ],
    )
    return pl.pallas_call(
        functools.partial(channelize_kernel, norm),
        grid_spec=grid_spec,
        out_shape=[
            jax.ShapeDtypeStruct(out_shape, jnp.bfloat16) for _ in range(split)
        ],
        compiler_params=pltpu.CompilerParams(vmem_limit_bytes=VMEM),
        cost_estimate=SMALL,
    )(odd, own, scale, got, rims, taps, table)


def correlate_kernel(weight, offsets, row_ref, *rest):
    out_ref, mixed, columns = rest[-3:]
    pieces = rest[: sum(len(arrays) for arrays in offsets)]
    rows, channels, _, inputs = out_ref.shape
    half_in = inputs // 2
    pairs, sides, _, depth, _ = pieces[0].shape
    deep = columns.shape[0]
    start = pl.multiple_of(row_ref[0], rows)

    def one_channel(c, carry):
        at = 0
        for arrays in offsets:
            for index, offset in enumerate(arrays):
                piece = pieces[at]
                at += 1
                for side in range(sides):
                    first = side * half_in + offset
                    for pair in range(pairs):
                        base = (index * pairs + pair) * depth
                        columns[base : base + depth, first : first + piece.shape[4]] = piece[
                            pair, side, c
                        ]
        left = columns[:, pl.ds(start, rows)].astype(jnp.float32) * weight
        parts = left.reshape(deep // depth, 2, depth // 2, rows)
        turned = jnp.stack([parts[:, 1], -parts[:, 0]], axis=1).reshape(deep, rows)
        for k in range(0, deep, LANES):
            mixed[k // LANES, pl.ds(0, rows, stride=2), :] = left[k : k + LANES].T
            mixed[k // LANES, pl.ds(1, rows, stride=2), :] = turned[k : k + LANES].T
        lhs = jnp.concatenate(
            [mixed[k].astype(jnp.bfloat16) for k in range(deep // LANES)], axis=1
        )
        product = jnp.dot(lhs, columns[...], preferred_element_type=jnp.float32)
        out_ref[:, c] = product.astype(jnp.bfloat16).reshape(rows, 2, inputs)
        return carry

    lax.fori_loop(0, channels, one_channel, 0)


def correlate(row_start, pieces, before, chunk, per, rows, count, inputs, weight):
    step = min(4, per)
    in_specs, operands, offsets = [], [row_start], []
    for offset, arrays in pieces:
        groups, channels, depth, width = arrays[0].shape
        skip = chunk * per % channels // step
        for array in arrays:
            operands.append(array.reshape(groups // 2, 2, channels, depth, width))
            in_specs.append(
                pl.BlockSpec(
                    (groups // 2, 2, step, depth, width),
                    lambda i, r, skip=skip: (0, 0, skip + i, 0, 0),
                )
            )
        offsets.append((offset,) * len(arrays))
    deep = len(pieces[0][1]) * groups // 2 * depth
    aliases = {}
    if before is not None:
        in_specs.append(pl.BlockSpec(memory_space=pl.ANY))
        operands.append(before)
        aliases = {len(operands) - 1: 0}
    first = chunk * per // step
    return pl.pallas_call(
        functools.partial(correlate_kernel, weight, offsets),
        grid_spec=pltpu.PrefetchScalarGridSpec(
            num_scalar_prefetch=1,
            grid=(per // step,),
            in_specs=in_specs,
            out_specs=pl.BlockSpec((rows, step, 2, inputs), lambda i, r: (0, first + i, 0, 0)),
            scratch_shapes=[
                pltpu.VMEM((deep // LANES, 2 * rows, LANES), jnp.float32),
                pltpu.VMEM((deep, inputs), jnp.bfloat16),
            ],
        ),
        out_shape=jax.ShapeDtypeStruct((rows, count, 2, inputs), jnp.bfloat16),
        input_output_aliases=aliases,
        compiler_params=pltpu.CompilerParams(vmem_limit_bytes=VMEM),
        cost_estimate=SMALL,
    )(*operands)


def after(value, *others):
    return lax.optimization_barrier((value, *others))[0]


def flipped(array, axis, bit):
    return lax.ppermute(array, axis, [(i, i ^ bit) for i in range(lax.axis_size(axis))])


def gather_steps(piece):
    steps, arrays = [], [piece]
    bit = lax.axis_size("half") // 2
    while bit:
        steps.append([flipped(array, "half", bit) for array in arrays])
        arrays = arrays + steps[-1]
        bit //= 2
    return arrays, steps


def per_device(voltages, scale_exps):
    volts = voltages[0]
    scale = jnp.exp2(scale_exps[0].astype(jnp.float32))
    blocks, _, count, inputs = volts.shape
    groups = lax.axis_size("freq")
    halves = lax.axis_size("half")
    half_in = inputs // 2
    odd = lax.axis_index("freq") % 2

    taps = jnp.broadcast_to(make_window(count).reshape(TAPS, count, 1), (TAPS, count, LANES))
    chunks = min(CHUNKS, count // groups)
    table = dft_table(count, groups, chunks)
    norm = 1.0 / (256.0 * math.sqrt(count))
    rim_start = blocks - (TAPS - 1)
    ahead = [(i, i + 2) for i in range(groups - 2)]

    def scaled(values, side, offset, width, first):
        start = side * half_in + offset
        picked = lax.dynamic_slice(
            values, (first, 0, 0, start), (blocks - first, 2, count, width)
        )
        factor = lax.dynamic_slice(scale, (first, start), (blocks - first, width))
        return (picked.astype(jnp.float32) * factor[:, None, None, :]).astype(jnp.bfloat16)

    widths = [half_in // 4, half_in // 4, half_in // 2]
    offsets = [sum(widths[:i]) for i in range(len(widths))]
    splits = [1, 2, 4]

    got, rims, spectra, edges = [], [], [], []
    for k, (offset, width) in enumerate(zip(offsets, widths)):
        give = volts if k == 0 else after(volts, got[k - 1], edges[k - 1], *rims[k - 2 : k - 1])
        got.append(flipped(scaled(give, 1 - odd, offset, width, 0), "freq", 1))
        own = scaled(volts, odd, offset, width, rim_start)
        edge = jnp.where(odd == 1, own, got[k][rim_start:])
        if k == 2:
            edge = after(edge, spectra[1][0])
        edges.append(edge)
        rims.append(lax.ppermute(edge, "freq", ahead))
        spectra.append(
            channelize(
                odd.reshape(1), volts, scale, got[k], rims[k], taps, table, groups, norm, offset,
                splits[k],
            )
        )

    units = [(k, array) for k, arrays in enumerate(spectra) for array in arrays]
    moved, steps = [], []
    for n, (k, array) in enumerate(units):
        ties = []
        if n == 1:
            ties += [rims[2]]
        if n == 2:
            ties += [spectra[2][0]]
        if n >= 3:
            ties += steps[n - 3][0] + [moved[n - 1][0]]
        if n >= 4:
            ties += steps[n - 4][-1]
        if ties:
            array = after(array, *ties)
        turned = lax.all_to_all(array, "freq", split_axis=0, concat_axis=0, tiled=True)
        arrays, step = gather_steps(turned)
        moved.append(arrays)
        steps.append(step)

    rows = inputs // halves
    row_start = (lax.axis_index("half") * rows).reshape(1)
    weight = 1.0 / (halves * groups * blocks)
    per = count // groups // chunks
    result = None
    for chunk in range(chunks):
        chosen, at = [], 0
        for offset, split in zip(offsets, splits):
            chosen.append((offset, moved[at + chunk * split // chunks]))
            at += split
        result = correlate(
            row_start, chosen, result, chunk, per, rows, count // groups, inputs, weight
        )
    return result


def solution(mesh):
    return jax.shard_map(
        per_device,
        mesh=mesh,
        in_specs=(P("half", "freq", None, None, None), P("half", "freq", None)),
        out_specs=P("half", "freq", None, None),
        check_vma=False,
    )
```

```python
import functools
import math

import jax
import jax.numpy as jnp
from jax import lax
from jax.experimental import pallas as pl
from jax.experimental.pallas import tpu as pltpu
from jax.sharding import PartitionSpec as P

TAPS = 4
CHUNKS = 4
LANES = 128
VMEM = 56 * 1024 * 1024


def make_window(count):
    steps = jnp.arange(TAPS * count, dtype=jnp.float32) + 0.5
    return jnp.sinc(steps / count - 2.0) * (
        0.5 - 0.5 * jnp.cos(2.0 * math.pi * steps / (TAPS * count))
    )


def dft_table(count, groups, chunks):
    per = count // (groups * chunks)
    index = jnp.arange(count, dtype=jnp.int32)
    channel = index.reshape(groups, chunks, per).transpose(1, 0, 2).reshape(count)
    angle = 2.0 * math.pi / count * (channel[:, None] * index[None, :] % count).astype(jnp.float32)
    cosine = jnp.cos(angle).astype(jnp.bfloat16)
    sine = jnp.sin(angle).astype(jnp.bfloat16)
    upper = jnp.concatenate([cosine, sine], axis=1).reshape(chunks, groups, 1, per, 2 * count)
    lower = jnp.concatenate([-sine, cosine], axis=1).reshape(chunks, groups, 1, per, 2 * count)
    return jnp.concatenate([upper, lower], axis=2).reshape(chunks, 2 * count // chunks, 2 * count)


def channelize_kernel(
    norm, odd_ref, own_ref, scale_ref, got_ref, rim_ref, taps_ref, table_ref, *rest
):
    outs, filtered, spread = rest[:-2], rest[-2], rest[-1]
    blocks, _, count, width = own_ref.shape
    times = 2 * blocks
    chunks, chunk_rows, _ = table_ref.shape
    odd = odd_ref[0] == 1

    def filter_rows(step, carry):
        rows = pl.ds(pl.multiple_of(step * 16, 16), 16)
        weights = [taps_ref[q, rows, :] for q in range(TAPS)]
        for part in range(2):
            for lane in range(0, width, LANES):
                lanes = slice(lane, lane + LANES)
                own = [
                    own_ref[b, part, rows, lanes].astype(jnp.float32) * scale_ref[b : b + 1, lanes]
                    for b in range(blocks)
                ]
                got = [got_ref[b, part, rows, lanes].astype(jnp.float32) for b in range(blocks)]
                line = [
                    rim_ref[b, part, rows, lanes].astype(jnp.float32) for b in range(TAPS - 1)
                ]
                line += [jnp.where(odd, g, o) for g, o in zip(got, own)]
                line += [jnp.where(odd, o, g) for g, o in zip(got, own)]
                at = pl.ds(pl.multiple_of(part * count + step * 16, 16), 16)
                for t in range(times):
                    total = weights[0] * line[t]
                    for q in range(1, TAPS):
                        total = total + weights[q] * line[t + q]
                    filtered[t, at, lanes] = total.astype(jnp.bfloat16)
        return carry

    lax.fori_loop(0, count // 16, filter_rows, 0)

    groups = outs[0].shape[0]
    depth = outs[0].shape[2]
    per = chunk_rows // (2 * groups)
    whole_table = table_ref[...].reshape(chunks * chunk_rows, 2 * count)

    def one_time(t, carry):
        spectrum = jnp.dot(whole_table, filtered[t], preferred_element_type=jnp.float32) * norm
        for block in range(chunks * groups):
            for part in range(2):
                first = (block * 2 + part) * per
                for lane in range(width // LANES):
                    spread[
                        lane, pl.ds(block * per * depth + part * times + t, per, stride=depth), :
                    ] = spectrum[first : first + per, lane * LANES : (lane + 1) * LANES]
        return carry

    lax.fori_loop(0, times, one_time, 0)

    for chunk in range(chunks):
        share = chunks // len(outs)
        out = outs[chunk // share]
        skip = chunk % share * per
        for group in range(groups):
            for c in range(per):
                base = ((chunk * groups + group) * per + c) * depth
                for lane in range(width // LANES):
                    out[group, skip + c, :, lane * LANES : (lane + 1) * LANES] = spread[
                        lane, base : base + depth, :
                    ].astype(jnp.bfloat16)


def channelize(odd, own, scale, got, rims, taps, table, groups, norm, offset, split):
    blocks, _, count, inputs = own.shape
    width = got.shape[3]
    tiles = inputs // 2 // width
    skip = offset // width
    chunks = table.shape[0]
    channels = count // groups // split
    depth = 4 * blocks
    out_shape = (groups, channels, depth, width)
    grid_spec = pltpu.PrefetchScalarGridSpec(
        num_scalar_prefetch=1,
        grid=(1,),
        in_specs=[
            pl.BlockSpec((blocks, 2, count, width), lambda i, o: (0, 0, 0, o[0] * tiles + skip)),
            pl.BlockSpec((blocks, width), lambda i, o: (0, o[0] * tiles + skip)),
            pl.BlockSpec((blocks, 2, count, width), lambda i, o: (0, 0, 0, 0)),
            pl.BlockSpec((TAPS - 1, 2, count, width), lambda i, o: (0, 0, 0, 0)),
            pl.BlockSpec((TAPS, count, LANES), lambda i, o: (0, 0, 0)),
            pl.BlockSpec(table.shape, lambda i, o: (0, 0, 0)),
        ],
        out_specs=[
            pl.BlockSpec(out_shape, lambda i, o: (0, 0, 0, 0))
            for _ in range(split)
        ],
        scratch_shapes=[
            pltpu.VMEM((2 * blocks, 2 * count, width), jnp.bfloat16),
            pltpu.VMEM((width // LANES, count * depth, LANES), jnp.float32),
        ],
    )
    return pl.pallas_call(
        functools.partial(channelize_kernel, norm),
        grid_spec=grid_spec,
        out_shape=[
            jax.ShapeDtypeStruct(out_shape, jnp.bfloat16) for _ in range(split)
        ],
        compiler_params=pltpu.CompilerParams(vmem_limit_bytes=VMEM),
        cost_estimate=pl.CostEstimate(
            flops=2 * (2 * blocks) * (2 * count) ** 2 * width,
            bytes_accessed=got.size * 8,
            transcendentals=0,
        ),
    )(odd, own, scale, got, rims, taps, table)


def correlate_kernel(weight, offsets, row_ref, *rest):
    out_ref, mixed, columns = rest[-3:]
    pieces = rest[: sum(len(arrays) for arrays in offsets)]
    rows, channels, _, inputs = out_ref.shape
    half_in = inputs // 2
    pairs, sides, _, depth, _ = pieces[0].shape
    deep = columns.shape[0]
    start = pl.multiple_of(row_ref[0], rows)

    def one_channel(c, carry):
        at = 0
        for arrays in offsets:
            for index, offset in enumerate(arrays):
                piece = pieces[at]
                at += 1
                for side in range(sides):
                    first = side * half_in + offset
                    for pair in range(pairs):
                        base = (index * pairs + pair) * depth
                        columns[base : base + depth, first : first + piece.shape[4]] = piece[
                            pair, side, c
                        ]
        left = columns[:, pl.ds(start, rows)].astype(jnp.float32) * weight
        parts = left.reshape(deep // depth, 2, depth // 2, rows)
        turned = jnp.stack([parts[:, 1], -parts[:, 0]], axis=1).reshape(deep, rows)
        for k in range(0, deep, LANES):
            mixed[k // LANES, pl.ds(0, rows, stride=2), :] = left[k : k + LANES].T
            mixed[k // LANES, pl.ds(1, rows, stride=2), :] = turned[k : k + LANES].T
        lhs = jnp.concatenate(
            [mixed[k].astype(jnp.bfloat16) for k in range(deep // LANES)], axis=1
        )
        product = jnp.dot(lhs, columns[...], preferred_element_type=jnp.float32)
        out_ref[:, c] = product.astype(jnp.bfloat16).reshape(rows, 2, inputs)
        return carry

    lax.fori_loop(0, channels, one_channel, 0)


def correlate(row_start, pieces, before, chunk, per, rows, count, inputs, weight):
    step = min(4, per)
    in_specs, operands, offsets = [], [row_start], []
    for offset, arrays in pieces:
        groups, channels, depth, width = arrays[0].shape
        skip = chunk * per % channels // step
        for array in arrays:
            operands.append(array.reshape(groups // 2, 2, channels, depth, width))
            in_specs.append(
                pl.BlockSpec(
                    (groups // 2, 2, step, depth, width),
                    lambda i, r, skip=skip: (0, 0, skip + i, 0, 0),
                )
            )
        offsets.append((offset,) * len(arrays))
    deep = len(pieces[0][1]) * groups // 2 * depth
    aliases = {}
    if before is not None:
        in_specs.append(pl.BlockSpec(memory_space=pl.ANY))
        operands.append(before)
        aliases = {len(operands) - 1: 0}
    first = chunk * per // step
    return pl.pallas_call(
        functools.partial(correlate_kernel, weight, offsets),
        grid_spec=pltpu.PrefetchScalarGridSpec(
            num_scalar_prefetch=1,
            grid=(per // step,),
            in_specs=in_specs,
            out_specs=pl.BlockSpec((rows, step, 2, inputs), lambda i, r: (0, first + i, 0, 0)),
            scratch_shapes=[
                pltpu.VMEM((deep // LANES, 2 * rows, LANES), jnp.float32),
                pltpu.VMEM((deep, inputs), jnp.bfloat16),
            ],
        ),
        out_shape=jax.ShapeDtypeStruct((rows, count, 2, inputs), jnp.bfloat16),
        input_output_aliases=aliases,
        compiler_params=pltpu.CompilerParams(vmem_limit_bytes=VMEM),
        cost_estimate=pl.CostEstimate(
            flops=2 * per * deep * 2 * rows * inputs,
            bytes_accessed=2 * (per * deep * inputs + rows * per * 2 * inputs),
            transcendentals=0,
        ),
    )(*operands)


def after(value, *others):
    return lax.optimization_barrier((value, *others))[0]


def flipped(array, axis, bit):
    return lax.ppermute(array, axis, [(i, i ^ bit) for i in range(lax.axis_size(axis))])


def gather_steps(piece):
    steps, arrays = [], [piece]
    bit = lax.axis_size("half") // 2
    while bit:
        steps.append([flipped(array, "half", bit) for array in arrays])
        arrays = arrays + steps[-1]
        bit //= 2
    return arrays, steps


def per_device(voltages, scale_exps):
    volts = voltages[0]
    scale = jnp.exp2(scale_exps[0].astype(jnp.float32))
    blocks, _, count, inputs = volts.shape
    groups = lax.axis_size("freq")
    halves = lax.axis_size("half")
    half_in = inputs // 2
    odd = lax.axis_index("freq") % 2

    taps = jnp.broadcast_to(make_window(count).reshape(TAPS, count, 1), (TAPS, count, LANES))
    chunks = min(CHUNKS, count // groups)
    table = dft_table(count, groups, chunks)
    norm = 1.0 / (256.0 * math.sqrt(count))
    rim_start = blocks - (TAPS - 1)
    ahead = [(i, i + 2) for i in range(groups - 2)]

    def scaled(values, side, offset, width, first):
        start = side * half_in + offset
        picked = lax.dynamic_slice(
            values, (first, 0, 0, start), (blocks - first, 2, count, width)
        )
        factor = lax.dynamic_slice(scale, (first, start), (blocks - first, width))
        return (picked.astype(jnp.float32) * factor[:, None, None, :]).astype(jnp.bfloat16)

    widths = [half_in // 4, half_in // 4, half_in // 2]
    offsets = [sum(widths[:i]) for i in range(len(widths))]
    splits = [1, 1, 4]

    got, rims, spectra, edges = [], [], [], []
    for k, (offset, width) in enumerate(zip(offsets, widths)):
        give = volts if k == 0 else after(volts, got[k - 1], edges[k - 1], *rims[k - 2 : k - 1])
        got.append(flipped(scaled(give, 1 - odd, offset, width, 0), "freq", 1))
        own = scaled(volts, odd, offset, width, rim_start)
        edge = jnp.where(odd == 1, own, got[k][rim_start:])
        if k == 0:
            edge = after(edge, table, taps)
        edges.append(edge)
        rims.append(lax.ppermute(edge, "freq", ahead))
        spectra.append(
            channelize(
                odd.reshape(1), volts, scale, got[k], rims[k], taps, table, groups, norm, offset,
                splits[k],
            )
        )

    units = [(k, array) for k, arrays in enumerate(spectra) for array in arrays]
    moved, steps = [], []
    for n, (k, array) in enumerate(units):
        ties = []
        if n == 0:
            ties += [rims[1]]
        if n >= 2:
            ties += [moved[n - 1][0]] + steps[n - 2][0]
        if n >= 3:
            ties += steps[n - 3][-1]
        if ties:
            array = after(array, *ties)
        turned = lax.all_to_all(array, "freq", split_axis=0, concat_axis=0, tiled=True)
        arrays, step = gather_steps(turned)
        moved.append(arrays)
        steps.append(step)

    rows = inputs // halves
    row_start = (lax.axis_index("half") * rows).reshape(1)
    weight = 1.0 / (halves * groups * blocks)
    per = count // groups // chunks
    result = None
    for chunk in range(chunks):
        chosen, at = [], 0
        for offset, split in zip(offsets, splits):
            chosen.append((offset, moved[at + chunk * split // chunks]))
            at += split
        result = correlate(
            row_start, chosen, result, chunk, per, rows, count // groups, inputs, weight
        )
    return result


def solution(mesh):
    return jax.shard_map(
        per_device,
        mesh=mesh,
        in_specs=(P("half", "freq", None, None, None), P("half", "freq", None)),
        out_specs=P("half", "freq", None, None),
        check_vma=False,
    )
```

```python
import functools
import math

import jax
import jax.numpy as jnp
from jax import lax
from jax.experimental import pallas as pl
from jax.experimental.pallas import tpu as pltpu
from jax.sharding import PartitionSpec as P

TAPS = 4
CHUNKS = 4
LANES = 128
VMEM = 56 * 1024 * 1024


def make_window(count):
    steps = jnp.arange(TAPS * count, dtype=jnp.float32) + 0.5
    return jnp.sinc(steps / count - 2.0) * (
        0.5 - 0.5 * jnp.cos(2.0 * math.pi * steps / (TAPS * count))
    )


def dft_table(count, groups, chunks):
    per = count // (groups * chunks)
    index = jnp.arange(count, dtype=jnp.int32)
    channel = index.reshape(groups, chunks, per).transpose(1, 0, 2).reshape(count)
    angle = 2.0 * math.pi / count * (channel[:, None] * index[None, :] % count).astype(jnp.float32)
    cosine = jnp.cos(angle).astype(jnp.bfloat16)
    sine = jnp.sin(angle).astype(jnp.bfloat16)
    upper = jnp.concatenate([cosine, sine], axis=1).reshape(chunks, groups, 1, per, 2 * count)
    lower = jnp.concatenate([-sine, cosine], axis=1).reshape(chunks, groups, 1, per, 2 * count)
    return jnp.concatenate([upper, lower], axis=2).reshape(chunks, 2 * count // chunks, 2 * count)


def channelize_kernel(
    norm, odd_ref, own_ref, scale_ref, got_ref, rim_ref, taps_ref, table_ref, *rest
):
    outs, filtered, spread = rest[:-2], rest[-2], rest[-1]
    blocks, _, count, width = own_ref.shape
    times = 2 * blocks
    chunks, chunk_rows, _ = table_ref.shape
    odd = odd_ref[0] == 1

    def filter_rows(step, carry):
        rows = pl.ds(pl.multiple_of(step * 16, 16), 16)
        weights = [taps_ref[q, rows, :] for q in range(TAPS)]
        for part in range(2):
            for lane in range(0, width, LANES):
                lanes = slice(lane, lane + LANES)
                own = [
                    own_ref[b, part, rows, lanes].astype(jnp.float32) * scale_ref[b : b + 1, lanes]
                    for b in range(blocks)
                ]
                got = [got_ref[b, part, rows, lanes].astype(jnp.float32) for b in range(blocks)]
                line = [
                    rim_ref[b, part, rows, lanes].astype(jnp.float32) for b in range(TAPS - 1)
                ]
                line += [jnp.where(odd, g, o) for g, o in zip(got, own)]
                line += [jnp.where(odd, o, g) for g, o in zip(got, own)]
                at = pl.ds(pl.multiple_of(part * count + step * 16, 16), 16)
                for t in range(times):
                    total = weights[0] * line[t]
                    for q in range(1, TAPS):
                        total = total + weights[q] * line[t + q]
                    filtered[t, at, lanes] = total.astype(jnp.bfloat16)
        return carry

    lax.fori_loop(0, count // 16, filter_rows, 0)

    groups = outs[0].shape[0]
    depth = outs[0].shape[2]
    per = chunk_rows // (2 * groups)
    whole_table = table_ref[...].reshape(chunks * chunk_rows, 2 * count)

    def one_time(t, carry):
        spectrum = jnp.dot(whole_table, filtered[t], preferred_element_type=jnp.float32) * norm
        for block in range(chunks * groups):
            for part in range(2):
                first = (block * 2 + part) * per
                for lane in range(width // LANES):
                    spread[
                        lane, pl.ds(block * per * depth + part * times + t, per, stride=depth), :
                    ] = spectrum[first : first + per, lane * LANES : (lane + 1) * LANES]
        return carry

    lax.fori_loop(0, times, one_time, 0)

    for chunk in range(chunks):
        share = chunks // len(outs)
        out = outs[chunk // share]
        skip = chunk % share * per
        for group in range(groups):
            for c in range(per):
                base = ((chunk * groups + group) * per + c) * depth
                for lane in range(width // LANES):
                    out[group, skip + c, :, lane * LANES : (lane + 1) * LANES] = spread[
                        lane, base : base + depth, :
                    ].astype(jnp.bfloat16)


def channelize(odd, own, scale, got, rims, taps, table, groups, norm, offset, inside, split):
    blocks, _, count, inputs = own.shape
    width = rims.shape[3]
    tiles = inputs // 2 // width
    skip = offset // width
    chunks = table.shape[0]
    channels = count // groups // split
    depth = 4 * blocks
    out_shape = (groups, channels, depth, width)
    grid_spec = pltpu.PrefetchScalarGridSpec(
        num_scalar_prefetch=1,
        grid=(1,),
        in_specs=[
            pl.BlockSpec((blocks, 2, count, width), lambda i, o: (0, 0, 0, o[0] * tiles + skip)),
            pl.BlockSpec((blocks, width), lambda i, o: (0, o[0] * tiles + skip)),
            pl.BlockSpec((blocks, 2, count, width), lambda i, o: (0, 0, 0, inside // width)),
            pl.BlockSpec((TAPS - 1, 2, count, width), lambda i, o: (0, 0, 0, 0)),
            pl.BlockSpec((TAPS, count, LANES), lambda i, o: (0, 0, 0)),
            pl.BlockSpec(table.shape, lambda i, o: (0, 0, 0)),
        ],
        out_specs=[
            pl.BlockSpec(out_shape, lambda i, o: (0, 0, 0, 0))
            for _ in range(split)
        ],
        scratch_shapes=[
            pltpu.VMEM((2 * blocks, 2 * count, width), jnp.bfloat16),
            pltpu.VMEM((width // LANES, count * depth, LANES), jnp.float32),
        ],
    )
    return pl.pallas_call(
        functools.partial(channelize_kernel, norm),
        grid_spec=grid_spec,
        out_shape=[
            jax.ShapeDtypeStruct(out_shape, jnp.bfloat16) for _ in range(split)
        ],
        compiler_params=pltpu.CompilerParams(vmem_limit_bytes=VMEM),
        cost_estimate=pl.CostEstimate(
            flops=2 * (2 * blocks) * (2 * count) ** 2 * width,
            bytes_accessed=rims.size * 10,
            transcendentals=0,
        ),
    )(odd, own, scale, got, rims, taps, table)


def correlate_kernel(weight, offsets, row_ref, *rest):
    out_ref, token_ref, mixed, columns = rest[-4:]
    token_ref[...] = jnp.zeros_like(token_ref)
    pieces = rest[: sum(len(arrays) for arrays in offsets)]
    rows, channels, _, inputs = out_ref.shape
    half_in = inputs // 2
    pairs, sides, _, depth, _ = pieces[0].shape
    deep = columns.shape[0]
    start = pl.multiple_of(row_ref[0], rows)

    def one_channel(c, carry):
        at = 0
        for arrays in offsets:
            for index, offset in enumerate(arrays):
                piece = pieces[at]
                at += 1
                for side in range(sides):
                    first = side * half_in + offset
                    for pair in range(pairs):
                        base = (index * pairs + pair) * depth
                        columns[base : base + depth, first : first + piece.shape[4]] = piece[
                            pair, side, c
                        ]
        left = columns[:, pl.ds(start, rows)].astype(jnp.float32) * weight
        parts = left.reshape(deep // depth, 2, depth // 2, rows)
        turned = jnp.stack([parts[:, 1], -parts[:, 0]], axis=1).reshape(deep, rows)
        for k in range(0, deep, LANES):
            mixed[k // LANES, pl.ds(0, rows, stride=2), :] = left[k : k + LANES].T
            mixed[k // LANES, pl.ds(1, rows, stride=2), :] = turned[k : k + LANES].T
        lhs = jnp.concatenate(
            [mixed[k].astype(jnp.bfloat16) for k in range(deep // LANES)], axis=1
        )
        product = jnp.dot(lhs, columns[...], preferred_element_type=jnp.float32)
        out_ref[:, c] = product.astype(jnp.bfloat16).reshape(rows, 2, inputs)
        return carry

    lax.fori_loop(0, channels, one_channel, 0)


def correlate(row_start, pieces, before, chunk, per, rows, count, inputs, weight):
    step = min(4, per)
    in_specs, operands, offsets = [], [row_start], []
    for offset, arrays in pieces:
        groups, channels, depth, width = arrays[0].shape
        skip = chunk * per % channels // step
        for array in arrays:
            operands.append(array.reshape(groups // 2, 2, channels, depth, width))
            in_specs.append(
                pl.BlockSpec(
                    (groups // 2, 2, step, depth, width),
                    lambda i, r, skip=skip: (0, 0, skip + i, 0, 0),
                )
            )
        offsets.append((offset,) * len(arrays))
    deep = len(pieces[0][1]) * groups // 2 * depth
    aliases = {}
    if before is not None:
        in_specs.append(pl.BlockSpec(memory_space=pl.ANY))
        operands.append(before)
        aliases = {len(operands) - 1: 0}
    first = chunk * per // step
    return pl.pallas_call(
        functools.partial(correlate_kernel, weight, offsets),
        grid_spec=pltpu.PrefetchScalarGridSpec(
            num_scalar_prefetch=1,
            grid=(per // step,),
            in_specs=in_specs,
            out_specs=[
                pl.BlockSpec((rows, step, 2, inputs), lambda i, r: (0, first + i, 0, 0)),
                pl.BlockSpec((8, LANES), lambda i, r: (0, 0)),
            ],
            scratch_shapes=[
                pltpu.VMEM((deep // LANES, 2 * rows, LANES), jnp.float32),
                pltpu.VMEM((deep, inputs), jnp.bfloat16),
            ],
        ),
        out_shape=[
            jax.ShapeDtypeStruct((rows, count, 2, inputs), jnp.bfloat16),
            jax.ShapeDtypeStruct((8, LANES), jnp.float32),
        ],
        input_output_aliases=aliases,
        compiler_params=pltpu.CompilerParams(vmem_limit_bytes=VMEM),
        cost_estimate=pl.CostEstimate(
            flops=2 * per * deep * 2 * rows * inputs,
            bytes_accessed=2 * (per * deep * inputs + rows * per * 2 * inputs),
            transcendentals=0,
        ),
    )(*operands)


def after_kernel(*refs):
    del refs


def after(value, *others):
    whole = pl.BlockSpec(memory_space=pl.ANY)
    return pl.pallas_call(
        after_kernel,
        in_specs=[whole] * (1 + len(others)),
        out_specs=whole,
        out_shape=jax.ShapeDtypeStruct(value.shape, value.dtype),
        input_output_aliases={0: 0},
    )(value, *others)


def flipped(array, axis, bit):
    return lax.ppermute(array, axis, [(i, i ^ bit) for i in range(lax.axis_size(axis))])


def gather_steps(piece, ties):
    steps, arrays = [], [piece]
    bit = lax.axis_size("half") // 2
    while bit:
        if ties and steps:
            arrays = [after(array, *ties) for array in arrays]
        steps.append([flipped(array, "half", bit) for array in arrays])
        arrays = arrays + steps[-1]
        bit //= 2
    return arrays, steps


def per_device(voltages, scale_exps):
    volts = voltages[0]
    scale = jnp.exp2(scale_exps[0].astype(jnp.float32))
    blocks, _, count, inputs = volts.shape
    groups = lax.axis_size("freq")
    halves = lax.axis_size("half")
    half_in = inputs // 2
    odd = lax.axis_index("freq") % 2

    taps = jnp.broadcast_to(make_window(count).reshape(TAPS, count, 1), (TAPS, count, LANES))
    chunks = min(CHUNKS, count // groups)
    table = dft_table(count, groups, chunks)
    norm = 1.0 / (256.0 * math.sqrt(count))
    rim_start = blocks - (TAPS - 1)
    ahead = [(i, i + 2) for i in range(groups - 2)]

    def scaled(side, offset, width, first, ties):
        start = side * half_in + offset
        picked = lax.dynamic_slice(
            volts, (first, 0, 0, start), (blocks - first, 2, count, width)
        )
        factor = lax.dynamic_slice(scale, (first, start), (blocks - first, width))
        if ties:
            factor = after(factor, *ties)
        return (picked.astype(jnp.float32) * factor[:, None, None, :]).astype(jnp.bfloat16)

    offsets = [half_in // 4 * 3, half_in // 2, 0]
    widths = [half_in // 4, half_in // 4, half_in // 2]
    splits = [1, 1, chunks]

    first = flipped(scaled(1 - odd, offsets[0], widths[0], 0, []), "freq", 1)
    ties = [first, table, taps]
    rest = flipped(scaled(1 - odd, 0, half_in - widths[0], 0, ties), "freq", 1)
    rims, spectra = [], []
    for k, (offset, width) in enumerate(zip(offsets, widths)):
        got, inside = (first, 0) if k == 0 else (rest, offset)
        own = scaled(odd, offset, width, rim_start, rims[k - 1 : k])
        edge = jnp.where(odd == 1, own, got[rim_start:, :, :, inside : inside + width])
        rims.append(lax.ppermute(edge, "freq", ahead))
        spectra.append(
            channelize(
                odd.reshape(1), volts, scale, got, rims[k], taps, table, groups, norm, offset,
                inside, splits[k],
            )
        )

    rows = inputs // halves
    row_start = (lax.axis_index("half") * rows).reshape(1)
    weight = 1.0 / (halves * groups * blocks)
    per = count // groups // chunks

    units = [array for arrays in spectra for array in arrays]
    moved, steps, tokens = [], [], []
    result = None
    for n, array in enumerate(units):
        ties = []
        if n >= 2:
            ties += [moved[n - 1][0]] + steps[n - 2 if n == 2 else n - 3][0]
        if n >= 3:
            ties += steps[n - 3][-1]
        if n == len(units) - 1:
            ties += tokens[:1]
        if ties:
            array = after(array, *ties)
        turned = lax.all_to_all(array, "freq", split_axis=0, concat_axis=0, tiled=True)
        if n == len(units) - 1 and len(tokens) > 1:
            turned = after(turned, tokens[1])
        arrays, step = gather_steps(turned, tokens[2:] if n == len(units) - 1 else [])
        moved.append(arrays)
        steps.append(step)
        chunk = n - len(units) + chunks
        if chunk >= 0:
            chosen = [(offsets[0], moved[0]), (offsets[1], moved[1]), (offsets[2], arrays)]
            result, token = correlate(
                row_start, chosen, result, chunk, per, rows, count // groups, inputs, weight
            )
            tokens.append(token)
    return result


def solution(mesh):
    return jax.shard_map(
        per_device,
        mesh=mesh,
        in_specs=(P("half", "freq", None, None, None), P("half", "freq", None)),
        out_specs=P("half", "freq", None, None),
        check_vma=False,
    )
```

```python
import functools
import math

import jax
import jax.numpy as jnp
from jax import lax
from jax.experimental import pallas as pl
from jax.experimental.pallas import tpu as pltpu
from jax.sharding import PartitionSpec as P

TAPS = 4
CHUNKS = 4
LANES = 128
VMEM = 56 * 1024 * 1024


def make_window(count):
    steps = jnp.arange(TAPS * count, dtype=jnp.float32) + 0.5
    return jnp.sinc(steps / count - 2.0) * (
        0.5 - 0.5 * jnp.cos(2.0 * math.pi * steps / (TAPS * count))
    )


def dft_table(count, groups, chunks):
    per = count // (groups * chunks)
    index = jnp.arange(count, dtype=jnp.int32)
    channel = index.reshape(groups, chunks, per).transpose(1, 0, 2).reshape(count)
    angle = 2.0 * math.pi / count * (channel[:, None] * index[None, :] % count).astype(jnp.float32)
    cosine = jnp.cos(angle).astype(jnp.bfloat16)
    sine = jnp.sin(angle).astype(jnp.bfloat16)
    upper = jnp.concatenate([cosine, sine], axis=1).reshape(chunks, groups, 1, per, 2 * count)
    lower = jnp.concatenate([-sine, cosine], axis=1).reshape(chunks, groups, 1, per, 2 * count)
    return jnp.concatenate([upper, lower], axis=2).reshape(chunks, 2 * count // chunks, 2 * count)


def channelize_kernel(
    norm, odd_ref, own_ref, scale_ref, got_ref, rim_ref, taps_ref, table_ref, *rest
):
    outs, filtered, spread = rest[:-2], rest[-2], rest[-1]
    blocks, _, count, width = own_ref.shape
    times = 2 * blocks
    chunks, chunk_rows, _ = table_ref.shape
    odd = odd_ref[0] == 1

    def filter_rows(step, carry):
        rows = pl.ds(pl.multiple_of(step * 16, 16), 16)
        weights = [taps_ref[q, rows, :] for q in range(TAPS)]
        for part in range(2):
            for lane in range(0, width, LANES):
                lanes = slice(lane, lane + LANES)
                own = [
                    own_ref[b, part, rows, lanes].astype(jnp.float32) * scale_ref[b : b + 1, lanes]
                    for b in range(blocks)
                ]
                got = [got_ref[b, part, rows, lanes].astype(jnp.float32) for b in range(blocks)]
                line = [
                    rim_ref[b, part, rows, lanes].astype(jnp.float32) for b in range(TAPS - 1)
                ]
                line += [jnp.where(odd, g, o) for g, o in zip(got, own)]
                line += [jnp.where(odd, o, g) for g, o in zip(got, own)]
                at = pl.ds(pl.multiple_of(part * count + step * 16, 16), 16)
                for t in range(times):
                    total = weights[0] * line[t]
                    for q in range(1, TAPS):
                        total = total + weights[q] * line[t + q]
                    filtered[t, at, lanes] = total.astype(jnp.bfloat16)
        return carry

    lax.fori_loop(0, count // 16, filter_rows, 0)

    groups = outs[0].shape[0]
    depth = outs[0].shape[2]
    per = chunk_rows // (2 * groups)
    whole_table = table_ref[...].reshape(chunks * chunk_rows, 2 * count)

    def one_time(t, carry):
        spectrum = jnp.dot(whole_table, filtered[t], preferred_element_type=jnp.float32) * norm
        for block in range(chunks * groups):
            for part in range(2):
                first = (block * 2 + part) * per
                for lane in range(width // LANES):
                    spread[
                        lane, pl.ds(block * per * depth + part * times + t, per, stride=depth), :
                    ] = spectrum[first : first + per, lane * LANES : (lane + 1) * LANES]
        return carry

    lax.fori_loop(0, times, one_time, 0)

    for chunk in range(chunks):
        share = chunks // len(outs)
        out = outs[chunk // share]
        skip = chunk % share * per
        for group in range(groups):
            for c in range(per):
                base = ((chunk * groups + group) * per + c) * depth
                for lane in range(width // LANES):
                    out[group, skip + c, :, lane * LANES : (lane + 1) * LANES] = spread[
                        lane, base : base + depth, :
                    ].astype(jnp.bfloat16)


def channelize(odd, own, scale, got, rims, taps, table, groups, norm, offset, split):
    blocks, _, count, inputs = own.shape
    width = rims.shape[3]
    tiles = inputs // 2 // width
    skip = offset // width
    chunks = table.shape[0]
    channels = count // groups // split
    depth = 4 * blocks
    out_shape = (groups, channels, depth, width)
    grid_spec = pltpu.PrefetchScalarGridSpec(
        num_scalar_prefetch=1,
        grid=(1,),
        in_specs=[
            pl.BlockSpec((blocks, 2, count, width), lambda i, o: (0, 0, 0, o[0] * tiles + skip)),
            pl.BlockSpec((blocks, width), lambda i, o: (0, o[0] * tiles + skip)),
            pl.BlockSpec((blocks, 2, count, width), lambda i, o: (0, 0, 0, 0)),
            pl.BlockSpec((TAPS - 1, 2, count, width), lambda i, o: (0, 0, 0, 0)),
            pl.BlockSpec((TAPS, count, LANES), lambda i, o: (0, 0, 0)),
            pl.BlockSpec(table.shape, lambda i, o: (0, 0, 0)),
        ],
        out_specs=[
            pl.BlockSpec(out_shape, lambda i, o: (0, 0, 0, 0))
            for _ in range(split)
        ],
        scratch_shapes=[
            pltpu.VMEM((2 * blocks, 2 * count, width), jnp.bfloat16),
            pltpu.VMEM((width // LANES, count * depth, LANES), jnp.float32),
        ],
    )
    return pl.pallas_call(
        functools.partial(channelize_kernel, norm),
        grid_spec=grid_spec,
        out_shape=[
            jax.ShapeDtypeStruct(out_shape, jnp.bfloat16) for _ in range(split)
        ],
        compiler_params=pltpu.CompilerParams(vmem_limit_bytes=VMEM),
        cost_estimate=pl.CostEstimate(
            flops=2 * (2 * blocks) * (2 * count) ** 2 * width,
            bytes_accessed=rims.size * 10,
            transcendentals=0,
        ),
    )(odd, own, scale, got, rims, taps, table)


def correlate_kernel(weight, offsets, row_ref, *rest):
    out_ref, token_ref, mixed, columns = rest[-4:]
    token_ref[...] = jnp.zeros_like(token_ref)
    pieces = rest[: sum(len(arrays) for arrays in offsets)]
    rows, channels, _, inputs = out_ref.shape
    half_in = inputs // 2
    pairs, sides, _, depth, _ = pieces[0].shape
    deep = columns.shape[0]
    start = pl.multiple_of(row_ref[0], rows)

    def one_channel(c, carry):
        at = 0
        for arrays in offsets:
            for index, offset in enumerate(arrays):
                piece = pieces[at]
                at += 1
                for side in range(sides):
                    first = side * half_in + offset
                    for pair in range(pairs):
                        base = (index * pairs + pair) * depth
                        columns[base : base + depth, first : first + piece.shape[4]] = piece[
                            pair, side, c
                        ]
        left = columns[:, pl.ds(start, rows)].astype(jnp.float32) * weight
        parts = left.reshape(deep // depth, 2, depth // 2, rows)
        turned = jnp.stack([parts[:, 1], -parts[:, 0]], axis=1).reshape(deep, rows)
        for k in range(0, deep, LANES):
            mixed[k // LANES, pl.ds(0, rows, stride=2), :] = left[k : k + LANES].T
            mixed[k // LANES, pl.ds(1, rows, stride=2), :] = turned[k : k + LANES].T
        lhs = jnp.concatenate(
            [mixed[k].astype(jnp.bfloat16) for k in range(deep // LANES)], axis=1
        )
        product = jnp.dot(lhs, columns[...], preferred_element_type=jnp.float32)
        out_ref[:, c] = product.astype(jnp.bfloat16).reshape(rows, 2, inputs)
        return carry

    lax.fori_loop(0, channels, one_channel, 0)


def correlate(row_start, pieces, before, chunk, per, rows, count, inputs, weight):
    step = min(4, per)
    in_specs, operands, offsets = [], [row_start], []
    for offset, arrays in pieces:
        groups, channels, depth, width = arrays[0].shape
        skip = chunk * per % channels // step
        for array in arrays:
            operands.append(array.reshape(groups // 2, 2, channels, depth, width))
            in_specs.append(
                pl.BlockSpec(
                    (groups // 2, 2, step, depth, width),
                    lambda i, r, skip=skip: (0, 0, skip + i, 0, 0),
                )
            )
        offsets.append((offset,) * len(arrays))
    deep = len(pieces[0][1]) * groups // 2 * depth
    aliases = {}
    if before is not None:
        in_specs.append(pl.BlockSpec(memory_space=pl.ANY))
        operands.append(before)
        aliases = {len(operands) - 1: 0}
    first = chunk * per // step
    return pl.pallas_call(
        functools.partial(correlate_kernel, weight, offsets),
        grid_spec=pltpu.PrefetchScalarGridSpec(
            num_scalar_prefetch=1,
            grid=(per // step,),
            in_specs=in_specs,
            out_specs=[
                pl.BlockSpec((rows, step, 2, inputs), lambda i, r: (0, first + i, 0, 0)),
                pl.BlockSpec((8, LANES), lambda i, r: (0, 0)),
            ],
            scratch_shapes=[
                pltpu.VMEM((deep // LANES, 2 * rows, LANES), jnp.float32),
                pltpu.VMEM((deep, inputs), jnp.bfloat16),
            ],
        ),
        out_shape=[
            jax.ShapeDtypeStruct((rows, count, 2, inputs), jnp.bfloat16),
            jax.ShapeDtypeStruct((8, LANES), jnp.float32),
        ],
        input_output_aliases=aliases,
        compiler_params=pltpu.CompilerParams(vmem_limit_bytes=VMEM),
        cost_estimate=pl.CostEstimate(
            flops=2 * per * deep * 2 * rows * inputs,
            bytes_accessed=2 * (per * deep * inputs + rows * per * 2 * inputs),
            transcendentals=0,
        ),
    )(*operands)


def after_kernel(*refs):
    del refs


def after(value, *others):
    whole = pl.BlockSpec(memory_space=pl.ANY)
    return pl.pallas_call(
        after_kernel,
        in_specs=[whole] * (1 + len(others)),
        out_specs=whole,
        out_shape=jax.ShapeDtypeStruct(value.shape, value.dtype),
        input_output_aliases={0: 0},
    )(value, *others)


def flipped(array, axis, bit):
    return lax.ppermute(array, axis, [(i, i ^ bit) for i in range(lax.axis_size(axis))])


def gather_steps(piece, ties):
    steps, arrays = [], [piece]
    bit = lax.axis_size("half") // 2
    while bit:
        if ties and steps:
            arrays = [after(array, *ties) for array in arrays]
        steps.append([flipped(array, "half", bit) for array in arrays])
        arrays = arrays + steps[-1]
        bit //= 2
    return arrays, steps


def per_device(voltages, scale_exps):
    volts = voltages[0]
    scale = jnp.exp2(scale_exps[0].astype(jnp.float32))
    blocks, _, count, inputs = volts.shape
    groups = lax.axis_size("freq")
    halves = lax.axis_size("half")
    half_in = inputs // 2
    odd = lax.axis_index("freq") % 2

    taps = jnp.broadcast_to(make_window(count).reshape(TAPS, count, 1), (TAPS, count, LANES))
    chunks = min(CHUNKS, count // groups)
    table = dft_table(count, groups, chunks)
    norm = 1.0 / (256.0 * math.sqrt(count))
    rim_start = blocks - (TAPS - 1)
    ahead = [(i, i + 2) for i in range(groups - 2)]

    def scaled(side, offset, width, first, ties):
        start = side * half_in + offset
        picked = lax.dynamic_slice(
            volts, (first, 0, 0, start), (blocks - first, 2, count, width)
        )
        factor = lax.dynamic_slice(scale, (first, start), (blocks - first, width))
        if ties:
            factor = after(factor, *ties)
        return (picked.astype(jnp.float32) * factor[:, None, None, :]).astype(jnp.bfloat16)

    offsets = [0, half_in // 4, half_in // 2]
    widths = [half_in // 4, half_in // 4, half_in // 2]
    splits = [1, 1, chunks]

    gives, got, rims, spectra = [], [], [], []
    for k, (offset, width) in enumerate(zip(offsets, widths)):
        ties = [[], [table, taps], []][k] + got[k - 1 : k]
        gives.append(scaled(1 - odd, offset, width, 0, ties))
        got.append(flipped(gives[k], "freq", 1))
    for k, (offset, width) in enumerate(zip(offsets, widths)):
        own = scaled(odd, offset, width, rim_start, rims[k - 1 : k])
        edge = jnp.where(odd == 1, own, got[k][rim_start:])
        rims.append(lax.ppermute(edge, "freq", ahead))
        spectra.append(
            channelize(
                odd.reshape(1), volts, scale, got[k], rims[k], taps, table, groups, norm, offset,
                splits[k],
            )
        )

    rows = inputs // halves
    row_start = (lax.axis_index("half") * rows).reshape(1)
    weight = 1.0 / (halves * groups * blocks)
    per = count // groups // chunks

    units = [array for arrays in spectra for array in arrays]
    moved, steps, tokens = [], [], []
    result = None
    for n, array in enumerate(units):
        ties = []
        if n == 0:
            ties += gives[-1:]
        if n >= 2:
            ties += [moved[n - 1][0]] + steps[n - 2 if n == 2 else n - 3][0]
        if n >= 3:
            ties += steps[n - 3][-1]
        if n == len(units) - 1:
            ties += tokens[:1]
        if ties:
            array = after(array, *ties)
        turned = lax.all_to_all(array, "freq", split_axis=0, concat_axis=0, tiled=True)
        if n == len(units) - 1 and len(tokens) > 1:
            turned = after(turned, tokens[1])
        arrays, step = gather_steps(turned, tokens[-1:])
        moved.append(arrays)
        steps.append(step)
        chunk = n - len(units) + chunks
        if chunk >= 0:
            chosen = [(offsets[0], moved[0]), (offsets[1], moved[1]), (offsets[2], arrays)]
            result, token = correlate(
                row_start, chosen, result, chunk, per, rows, count // groups, inputs, weight
            )
            tokens.append(token)
    return result


def solution(mesh):
    return jax.shard_map(
        per_device,
        mesh=mesh,
        in_specs=(P("half", "freq", None, None, None), P("half", "freq", None)),
        out_specs=P("half", "freq", None, None),
        check_vma=False,
    )
```

```python
import functools
import math

import jax
import jax.numpy as jnp
from jax import lax
from jax.experimental import pallas as pl
from jax.experimental.pallas import tpu as pltpu
from jax.sharding import PartitionSpec as P

TAPS = 4
CHUNKS = 4
LANES = 128
VMEM = 56 * 1024 * 1024


def make_window(count):
    steps = jnp.arange(TAPS * count, dtype=jnp.float32) + 0.5
    return jnp.sinc(steps / count - 2.0) * (
        0.5 - 0.5 * jnp.cos(2.0 * math.pi * steps / (TAPS * count))
    )


def dft_table(count, groups, chunks):
    per = count // (groups * chunks)
    index = jnp.arange(count, dtype=jnp.int32)
    channel = index.reshape(groups, chunks, per).transpose(1, 0, 2).reshape(count)
    angle = 2.0 * math.pi / count * (channel[:, None] * index[None, :] % count).astype(jnp.float32)
    cosine = jnp.cos(angle).astype(jnp.bfloat16)
    sine = jnp.sin(angle).astype(jnp.bfloat16)
    upper = jnp.concatenate([cosine, sine], axis=1).reshape(chunks, groups, 1, per, 2 * count)
    lower = jnp.concatenate([-sine, cosine], axis=1).reshape(chunks, groups, 1, per, 2 * count)
    return jnp.concatenate([upper, lower], axis=2).reshape(chunks, 2 * count // chunks, 2 * count)


def channelize_kernel(norm, parts, odd_ref, own_ref, scale_ref, *rest):
    got_refs, rim_refs = rest[:parts], rest[parts : 2 * parts]
    taps_ref, table_ref = rest[2 * parts : 2 * parts + 2]
    outs, filtered, spread = rest[2 * parts + 2 : -2], rest[-2], rest[-1]
    blocks, _, count, width = own_ref.shape
    times = 2 * blocks
    chunks, chunk_rows, _ = table_ref.shape
    together = filtered.shape[2] // width
    part_width = width // parts
    odd = odd_ref[0] == 1

    def filter_rows(step, carry):
        rows = pl.ds(pl.multiple_of(step * 16, 16), 16)
        weights = [taps_ref[q, rows, :] for q in range(TAPS)]
        for part in range(2):
            for lane in range(0, width, LANES):
                lanes = slice(lane, lane + LANES)
                got_ref, rim_ref = got_refs[lane // part_width], rim_refs[lane // part_width]
                inner = slice(lane % part_width, lane % part_width + LANES)
                own = [
                    own_ref[b, part, rows, lanes].astype(jnp.float32) * scale_ref[b : b + 1, lanes]
                    for b in range(blocks)
                ]
                got = [got_ref[b, part, rows, inner].astype(jnp.float32) for b in range(blocks)]
                line = [
                    rim_ref[b, part, rows, inner].astype(jnp.float32) for b in range(TAPS - 1)
                ]
                line += [jnp.where(odd, g, o) for g, o in zip(got, own)]
                line += [jnp.where(odd, o, g) for g, o in zip(got, own)]
                at = pl.ds(pl.multiple_of(part * count + step * 16, 16), 16)
                for t in range(times):
                    total = weights[0] * line[t]
                    for q in range(1, TAPS):
                        total = total + weights[q] * line[t + q]
                    place = t % together * width + lane
                    filtered[t // together, at, place : place + LANES] = total.astype(jnp.bfloat16)
        return carry

    lax.fori_loop(0, count // 16, filter_rows, 0)

    groups = outs[0].shape[0]
    depth = outs[0].shape[2]
    per = chunk_rows // (2 * groups)
    whole_table = table_ref[...].reshape(chunks * chunk_rows, 2 * count)

    def some_times(step, carry):
        spectrum = jnp.dot(whole_table, filtered[step], preferred_element_type=jnp.float32) * norm
        for block in range(chunks * groups):
            for part in range(2):
                first = (block * 2 + part) * per
                for place in range(0, together * width, LANES):
                    t = step * together + place // width
                    spread[
                        place % width // LANES,
                        pl.ds(block * per * depth + part * times + t, per, stride=depth),
                        :,
                    ] = spectrum[first : first + per, place : place + LANES]
        return carry

    lax.fori_loop(0, times // together, some_times, 0)

    for chunk in range(chunks):
        share = chunks // len(outs)
        out = outs[chunk // share]
        skip = chunk % share * per
        for group in range(groups):
            for c in range(per):
                base = ((chunk * groups + group) * per + c) * depth
                for lane in range(width // LANES):
                    out[group, skip + c, :, lane * LANES : (lane + 1) * LANES] = spread[
                        lane, base : base + depth, :
                    ].astype(jnp.bfloat16)


def channelize(odd, own, scale, got, rims, taps, table, groups, norm, offset, split):
    blocks, _, count, inputs = own.shape
    parts = len(got)
    part_width = got[0].shape[3]
    width = parts * part_width
    tiles = inputs // 2 // width
    skip = offset // width
    chunks = table.shape[0]
    channels = count // groups // split
    depth = 4 * blocks
    together = max(1, 256 // width)
    out_shape = (groups, channels, depth, width)
    grid_spec = pltpu.PrefetchScalarGridSpec(
        num_scalar_prefetch=1,
        grid=(1,),
        in_specs=[
            pl.BlockSpec((blocks, 2, count, width), lambda i, o: (0, 0, 0, o[0] * tiles + skip)),
            pl.BlockSpec((blocks, width), lambda i, o: (0, o[0] * tiles + skip)),
        ]
        + [pl.BlockSpec((blocks, 2, count, part_width), lambda i, o: (0, 0, 0, 0))] * parts
        + [pl.BlockSpec((TAPS - 1, 2, count, part_width), lambda i, o: (0, 0, 0, 0))] * parts
        + [
            pl.BlockSpec((TAPS, count, LANES), lambda i, o: (0, 0, 0)),
            pl.BlockSpec(table.shape, lambda i, o: (0, 0, 0)),
        ],
        out_specs=[pl.BlockSpec(out_shape, lambda i, o: (0, 0, 0, 0)) for _ in range(split)],
        scratch_shapes=[
            pltpu.VMEM((2 * blocks // together, 2 * count, together * width), jnp.bfloat16),
            pltpu.VMEM((width // LANES, count * depth, LANES), jnp.float32),
        ],
    )
    return pl.pallas_call(
        functools.partial(channelize_kernel, norm, parts),
        grid_spec=grid_spec,
        out_shape=[jax.ShapeDtypeStruct(out_shape, jnp.bfloat16) for _ in range(split)],
        compiler_params=pltpu.CompilerParams(vmem_limit_bytes=VMEM),
        cost_estimate=pl.CostEstimate(
            flops=2 * (2 * blocks) * (2 * count) ** 2 * width,
            bytes_accessed=6 * blocks * count * width * 4,
            transcendentals=0,
        ),
    )(odd, own, scale, *got, *rims, taps, table)


def correlate_kernel(weight, layout, row_ref, *rest):
    out_ref, token_ref, mixed, columns = rest[-4:]
    token_ref[...] = jnp.zeros_like(token_ref)
    rows, channels, _, inputs = out_ref.shape
    half_in = inputs // 2
    deep = columns.shape[0]
    start = pl.multiple_of(row_ref[0], rows)
    me = row_ref[1]

    def one_channel(c, carry):
        at = 0
        for offset, masks, gathered in layout:
            for index, mask in enumerate(masks):
                piece = rest[at]
                if gathered:
                    piece = piece.at[me ^ mask]
                else:
                    at += 1
                pairs, sides, _, depth, width = piece.shape
                for side in range(sides):
                    first = side * half_in + offset
                    for pair in range(pairs):
                        base = (index * pairs + pair) * depth
                        columns[base : base + depth, first : first + width] = piece[pair, side, c]
            if gathered:
                at += 1
        left = columns[:, pl.ds(start, rows)].astype(jnp.float32) * weight
        parts = left.reshape(deep // depth, 2, depth // 2, rows)
        turned = jnp.stack([parts[:, 1], -parts[:, 0]], axis=1).reshape(deep, rows)
        for k in range(0, deep, LANES):
            mixed[k // LANES, pl.ds(0, rows, stride=2), :] = left[k : k + LANES].T
            mixed[k // LANES, pl.ds(1, rows, stride=2), :] = turned[k : k + LANES].T
        lhs = jnp.concatenate(
            [mixed[k].astype(jnp.bfloat16) for k in range(deep // LANES)], axis=1
        )
        product = jnp.dot(lhs, columns[...], preferred_element_type=jnp.float32)
        out_ref[:, c] = product.astype(jnp.bfloat16).reshape(rows, 2, inputs)
        return carry

    lax.fori_loop(0, channels, one_channel, 0)


def correlate(row_start, pieces, before, chunk, per, rows, count, inputs, weight):
    step = min(4, per)
    in_specs, operands, layout = [], [row_start], []
    masks = segment_masks()
    for offset, arrays in pieces:
        gathered = not isinstance(arrays, list)
        for array in [arrays] if gathered else arrays:
            groups, channels, depth, width = array.shape[-4:]
            skip = chunk * per % channels // step
            lead = array.shape[:-4]
            operands.append(array.reshape(*lead, groups // 2, 2, channels, depth, width))
            in_specs.append(
                pl.BlockSpec(
                    (*lead, groups // 2, 2, step, depth, width),
                    lambda i, r, skip=skip, zeros=(0,) * len(lead): (*zeros, 0, 0, skip + i, 0, 0),
                )
            )
        layout.append((offset, masks, gathered))
    deep = len(masks) * groups // 2 * depth
    aliases = {}
    if before is not None:
        in_specs.append(pl.BlockSpec(memory_space=pl.ANY))
        operands.append(before)
        aliases = {len(operands) - 1: 0}
    first = chunk * per // step
    return pl.pallas_call(
        functools.partial(correlate_kernel, weight, layout),
        grid_spec=pltpu.PrefetchScalarGridSpec(
            num_scalar_prefetch=1,
            grid=(per // step,),
            in_specs=in_specs,
            out_specs=[
                pl.BlockSpec((rows, step, 2, inputs), lambda i, r: (0, first + i, 0, 0)),
                pl.BlockSpec((8, LANES), lambda i, r: (0, 0)),
            ],
            scratch_shapes=[
                pltpu.VMEM((deep // LANES, 2 * rows, LANES), jnp.float32),
                pltpu.VMEM((deep, inputs), jnp.bfloat16),
            ],
        ),
        out_shape=[
            jax.ShapeDtypeStruct((rows, count, 2, inputs), jnp.bfloat16),
            jax.ShapeDtypeStruct((8, LANES), jnp.float32),
        ],
        input_output_aliases=aliases,
        compiler_params=pltpu.CompilerParams(vmem_limit_bytes=VMEM),
        cost_estimate=pl.CostEstimate(
            flops=2 * per * deep * 2 * rows * inputs,
            bytes_accessed=2 * (per * deep * inputs + rows * per * 2 * inputs),
            transcendentals=0,
        ),
    )(*operands)


def segment_masks():
    masks = [0]
    bit = lax.axis_size("half") // 2
    while bit:
        masks += [mask ^ bit for mask in masks]
        bit //= 2
    return masks


def after_kernel(*refs):
    del refs


def after(value, *others):
    whole = pl.BlockSpec(memory_space=pl.ANY)
    return pl.pallas_call(
        after_kernel,
        in_specs=[whole] * (1 + len(others)),
        out_specs=whole,
        out_shape=jax.ShapeDtypeStruct(value.shape, value.dtype),
        input_output_aliases={0: 0},
    )(value, *others)


def flipped(array, axis, bit):
    return lax.ppermute(array, axis, [(i, i ^ bit) for i in range(lax.axis_size(axis))])


def gather_steps(piece, ties):
    steps, arrays = [], [piece]
    bit = lax.axis_size("half") // 2
    while bit:
        if ties and steps:
            arrays = [after(array, *ties) for array in arrays]
        steps.append([flipped(array, "half", bit) for array in arrays])
        arrays = arrays + steps[-1]
        bit //= 2
    return arrays, steps


def per_device(voltages, scale_exps):
    volts = voltages[0]
    scale = jnp.exp2(scale_exps[0].astype(jnp.float32))
    blocks, _, count, inputs = volts.shape
    groups = lax.axis_size("freq")
    halves = lax.axis_size("half")
    half_in = inputs // 2
    odd = lax.axis_index("freq") % 2

    taps = jnp.broadcast_to(make_window(count).reshape(TAPS, count, 1), (TAPS, count, LANES))
    chunks = min(CHUNKS, count // groups)
    table = dft_table(count, groups, chunks)
    norm = 1.0 / (256.0 * math.sqrt(count))
    rim_start = blocks - (TAPS - 1)
    ahead = [(i, i + 2) for i in range(groups - 2)]

    def scaled(side, offset, width, first, ties):
        start = side * half_in + offset
        picked = lax.dynamic_slice(
            volts, (first, 0, 0, start), (blocks - first, 2, count, width)
        )
        factor = lax.dynamic_slice(scale, (first, start), (blocks - first, width))
        if ties:
            factor = after(factor, *ties)
        return (picked.astype(jnp.float32) * factor[:, None, None, :]).astype(jnp.bfloat16)

    piece_width = half_in // 4
    starts = [piece_width * k for k in range(4)]
    gives, got, rims = [], [], []
    for k, start in enumerate(starts):
        ties = ([table, taps] if k == 1 else []) + got[k - 1 : k]
        gives.append(scaled(1 - odd, start, piece_width, 0, ties))
        got.append(flipped(gives[k], "freq", 1))
    for k, start in enumerate(starts):
        own = scaled(odd, start, piece_width, rim_start, rims[k - 1 : k])
        rims.append(
            lax.ppermute(jnp.where(odd == 1, own, got[k][rim_start:]), "freq", ahead)
        )

    def transformed(first, last, split):
        return channelize(
            odd.reshape(1), volts, scale, got[first:last], rims[first:last], taps, table, groups,
            norm, starts[first], split,
        )

    def exchanged(array):
        return lax.all_to_all(array, "freq", split_axis=0, concat_axis=0, tiled=True)

    rows = inputs // halves
    half = lax.axis_index("half")
    row_start = jnp.stack([half * rows, half])
    weight = 1.0 / (halves * groups * blocks)
    per = count // groups // chunks

    early = []
    for k in range(2):
        array = after(transformed(k, k + 1, 1)[0], got[k + 2], rims[k + 1])
        early.append((starts[k], lax.all_gather(exchanged(array), "half", axis=0)))
    result, tokens = None, []
    for chunk, array in enumerate(transformed(2, 4, chunks)):
        turned = exchanged(array)
        if chunk > 1 and chunk == chunks - 1:
            turned = after(turned, tokens[1])
        arrays, _ = gather_steps(turned, tokens[-1:])
        result, token = correlate(
            row_start, early + [(starts[2], arrays)], result, chunk, per, rows, count // groups,
            inputs, weight,
        )
        tokens.append(token)
    return result


def solution(mesh):
    return jax.shard_map(
        per_device,
        mesh=mesh,
        in_specs=(P("half", "freq", None, None, None), P("half", "freq", None)),
        out_specs=P("half", "freq", None, None),
        check_vma=False,
    )
```

```python
import functools
import math

import jax
import jax.numpy as jnp
from jax import lax
from jax.experimental import pallas as pl
from jax.experimental.pallas import tpu as pltpu
from jax.sharding import PartitionSpec as P

TAPS = 4
CHUNKS = 4
LANES = 128
VMEM = 56 * 1024 * 1024


def make_window(count):
    steps = jnp.arange(TAPS * count, dtype=jnp.float32) + 0.5
    return jnp.sinc(steps / count - 2.0) * (
        0.5 - 0.5 * jnp.cos(2.0 * math.pi * steps / (TAPS * count))
    )


def dft_table(count, groups, chunks):
    per = count // (groups * chunks)
    index = jnp.arange(count, dtype=jnp.int32)
    channel = index.reshape(groups, chunks, per).transpose(1, 0, 2).reshape(count)
    angle = 2.0 * math.pi / count * (channel[:, None] * index[None, :] % count).astype(jnp.float32)
    cosine = jnp.cos(angle).astype(jnp.bfloat16)
    sine = jnp.sin(angle).astype(jnp.bfloat16)
    upper = jnp.concatenate([cosine, sine], axis=1).reshape(chunks, groups, 1, per, 2 * count)
    lower = jnp.concatenate([-sine, cosine], axis=1).reshape(chunks, groups, 1, per, 2 * count)
    return jnp.concatenate([upper, lower], axis=2).reshape(chunks, 2 * count // chunks, 2 * count)


def channelize_kernel(norm, parts, odd_ref, own_ref, scale_ref, *rest):
    got_refs, rim_refs = rest[:parts], rest[parts : 2 * parts]
    taps_ref, table_ref = rest[2 * parts : 2 * parts + 2]
    outs, filtered, spread = rest[2 * parts + 2 : -2], rest[-2], rest[-1]
    blocks, _, count, width = own_ref.shape
    times = 2 * blocks
    chunks, chunk_rows, _ = table_ref.shape
    together = filtered.shape[2] // width
    part_width = width // parts
    odd = odd_ref[0] == 1

    def filter_rows(step, carry):
        rows = pl.ds(pl.multiple_of(step * 16, 16), 16)
        weights = [taps_ref[q, rows, :] for q in range(TAPS)]
        for part in range(2):
            for lane in range(0, width, LANES):
                lanes = slice(lane, lane + LANES)
                got_ref, rim_ref = got_refs[lane // part_width], rim_refs[lane // part_width]
                inner = slice(lane % part_width, lane % part_width + LANES)
                own = [
                    own_ref[b, part, rows, lanes].astype(jnp.float32) * scale_ref[b : b + 1, lanes]
                    for b in range(blocks)
                ]
                got = [got_ref[b, part, rows, inner].astype(jnp.float32) for b in range(blocks)]
                line = [
                    rim_ref[b, part, rows, inner].astype(jnp.float32) for b in range(TAPS - 1)
                ]
                line += [jnp.where(odd, g, o) for g, o in zip(got, own)]
                line += [jnp.where(odd, o, g) for g, o in zip(got, own)]
                at = pl.ds(pl.multiple_of(part * count + step * 16, 16), 16)
                for t in range(times):
                    total = weights[0] * line[t]
                    for q in range(1, TAPS):
                        total = total + weights[q] * line[t + q]
                    place = t % together * width + lane
                    filtered[t // together, at, place : place + LANES] = total.astype(jnp.bfloat16)
        return carry

    lax.fori_loop(0, count // 16, filter_rows, 0)

    groups = outs[0].shape[0]
    depth = outs[0].shape[2]
    per = chunk_rows // (2 * groups)
    whole_table = table_ref[...].reshape(chunks * chunk_rows, 2 * count)

    def some_times(step, carry):
        spectrum = jnp.dot(whole_table, filtered[step], preferred_element_type=jnp.float32) * norm
        for block in range(chunks * groups):
            for part in range(2):
                first = (block * 2 + part) * per
                for place in range(0, together * width, LANES):
                    t = step * together + place // width
                    spread[
                        place % width // LANES,
                        pl.ds(block * per * depth + part * times + t, per, stride=depth),
                        :,
                    ] = spectrum[first : first + per, place : place + LANES]
        return carry

    lax.fori_loop(0, times // together, some_times, 0)

    for chunk in range(chunks):
        share = chunks // len(outs)
        out = outs[chunk // share]
        skip = chunk % share * per
        for group in range(groups):
            for c in range(per):
                base = ((chunk * groups + group) * per + c) * depth
                for lane in range(width // LANES):
                    out[group, skip + c, :, lane * LANES : (lane + 1) * LANES] = spread[
                        lane, base : base + depth, :
                    ].astype(jnp.bfloat16)


def channelize(odd, own, scale, got, rims, taps, table, groups, norm, offset, split):
    blocks, _, count, inputs = own.shape
    parts = len(got)
    part_width = got[0].shape[3]
    width = parts * part_width
    tiles = inputs // 2 // width
    skip = offset // width
    chunks = table.shape[0]
    channels = count // groups // split
    depth = 4 * blocks
    together = max(1, 256 // width)
    out_shape = (groups, channels, depth, width)
    grid_spec = pltpu.PrefetchScalarGridSpec(
        num_scalar_prefetch=1,
        grid=(1,),
        in_specs=[
            pl.BlockSpec((blocks, 2, count, width), lambda i, o: (0, 0, 0, o[0] * tiles + skip)),
            pl.BlockSpec((blocks, width), lambda i, o: (0, o[0] * tiles + skip)),
        ]
        + [pl.BlockSpec((blocks, 2, count, part_width), lambda i, o: (0, 0, 0, 0))] * parts
        + [pl.BlockSpec((TAPS - 1, 2, count, part_width), lambda i, o: (0, 0, 0, 0))] * parts
        + [
            pl.BlockSpec((TAPS, count, LANES), lambda i, o: (0, 0, 0)),
            pl.BlockSpec(table.shape, lambda i, o: (0, 0, 0)),
        ],
        out_specs=[pl.BlockSpec(out_shape, lambda i, o: (0, 0, 0, 0)) for _ in range(split)],
        scratch_shapes=[
            pltpu.VMEM((2 * blocks // together, 2 * count, together * width), jnp.bfloat16),
            pltpu.VMEM((width // LANES, count * depth, LANES), jnp.float32),
        ],
    )
    return pl.pallas_call(
        functools.partial(channelize_kernel, norm, parts),
        grid_spec=grid_spec,
        out_shape=[jax.ShapeDtypeStruct(out_shape, jnp.bfloat16) for _ in range(split)],
        compiler_params=pltpu.CompilerParams(vmem_limit_bytes=VMEM),
        cost_estimate=pl.CostEstimate(
            flops=2 * (2 * blocks) * (2 * count) ** 2 * width,
            bytes_accessed=6 * blocks * count * width * 4,
            transcendentals=0,
        ),
    )(odd, own, scale, *got, *rims, taps, table)


def correlate_kernel(weight, layout, row_ref, *rest):
    out_ref, token_ref, mixed, columns = rest[-4:]
    token_ref[...] = jnp.zeros_like(token_ref)
    rows, channels, _, inputs = out_ref.shape
    half_in = inputs // 2
    deep = columns.shape[0]
    start = pl.multiple_of(row_ref[0], rows)
    me = row_ref[1]

    def one_channel(c, carry):
        at = 0
        for offset, masks, gathered in layout:
            for index, mask in enumerate(masks):
                piece = rest[at]
                if gathered:
                    piece = piece.at[me ^ mask]
                else:
                    at += 1
                pairs, sides, _, depth, width = piece.shape
                for side in range(sides):
                    first = side * half_in + offset
                    for pair in range(pairs):
                        base = (index * pairs + pair) * depth
                        columns[base : base + depth, first : first + width] = piece[pair, side, c]
            if gathered:
                at += 1
        left = columns[:, pl.ds(start, rows)].astype(jnp.float32) * weight
        parts = left.reshape(deep // depth, 2, depth // 2, rows)
        turned = jnp.stack([parts[:, 1], -parts[:, 0]], axis=1).reshape(deep, rows)
        for k in range(0, deep, LANES):
            mixed[k // LANES, pl.ds(0, rows, stride=2), :] = left[k : k + LANES].T
            mixed[k // LANES, pl.ds(1, rows, stride=2), :] = turned[k : k + LANES].T
        lhs = jnp.concatenate(
            [mixed[k].astype(jnp.bfloat16) for k in range(deep // LANES)], axis=1
        )
        product = jnp.dot(lhs, columns[...], preferred_element_type=jnp.float32)
        out_ref[:, c] = product.astype(jnp.bfloat16).reshape(rows, 2, inputs)
        return carry

    lax.fori_loop(0, channels, one_channel, 0)


def correlate(row_start, pieces, before, chunk, per, rows, count, inputs, weight):
    step = min(4, per)
    in_specs, operands, layout = [], [row_start], []
    masks = segment_masks()
    for offset, arrays in pieces:
        gathered = not isinstance(arrays, list)
        for array in [arrays] if gathered else arrays:
            groups, channels, depth, width = array.shape[-4:]
            skip = chunk * per % channels // step
            lead = array.shape[:-4]
            operands.append(array.reshape(*lead, groups // 2, 2, channels, depth, width))
            in_specs.append(
                pl.BlockSpec(
                    (*lead, groups // 2, 2, step, depth, width),
                    lambda i, r, skip=skip, zeros=(0,) * len(lead): (*zeros, 0, 0, skip + i, 0, 0),
                )
            )
        layout.append((offset, masks, gathered))
    deep = len(masks) * groups // 2 * depth
    aliases = {}
    if before is not None:
        in_specs.append(pl.BlockSpec(memory_space=pl.ANY))
        operands.append(before)
        aliases = {len(operands) - 1: 0}
    first = chunk * per // step
    return pl.pallas_call(
        functools.partial(correlate_kernel, weight, layout),
        grid_spec=pltpu.PrefetchScalarGridSpec(
            num_scalar_prefetch=1,
            grid=(per // step,),
            in_specs=in_specs,
            out_specs=[
                pl.BlockSpec((rows, step, 2, inputs), lambda i, r: (0, first + i, 0, 0)),
                pl.BlockSpec((8, LANES), lambda i, r: (0, 0)),
            ],
            scratch_shapes=[
                pltpu.VMEM((deep // LANES, 2 * rows, LANES), jnp.float32),
                pltpu.VMEM((deep, inputs), jnp.bfloat16),
            ],
        ),
        out_shape=[
            jax.ShapeDtypeStruct((rows, count, 2, inputs), jnp.bfloat16),
            jax.ShapeDtypeStruct((8, LANES), jnp.float32),
        ],
        input_output_aliases=aliases,
        compiler_params=pltpu.CompilerParams(vmem_limit_bytes=VMEM),
        cost_estimate=pl.CostEstimate(
            flops=2 * per * deep * 2 * rows * inputs,
            bytes_accessed=2 * (per * deep * inputs + rows * per * 2 * inputs),
            transcendentals=0,
        ),
    )(*operands)


def segment_masks():
    masks = [0]
    bit = lax.axis_size("half") // 2
    while bit:
        masks += [mask ^ bit for mask in masks]
        bit //= 2
    return masks


def after_kernel(*refs):
    del refs


def after(value, *others):
    whole = pl.BlockSpec(memory_space=pl.ANY)
    return pl.pallas_call(
        after_kernel,
        in_specs=[whole] * (1 + len(others)),
        out_specs=whole,
        out_shape=jax.ShapeDtypeStruct(value.shape, value.dtype),
        input_output_aliases={0: 0},
    )(value, *others)


def flipped(array, axis, bit):
    return lax.ppermute(array, axis, [(i, i ^ bit) for i in range(lax.axis_size(axis))])


def gather_steps(piece, ties):
    steps, arrays = [], [piece]
    bit = lax.axis_size("half") // 2
    while bit:
        if ties and steps:
            arrays = [after(array, *ties) for array in arrays]
        steps.append([flipped(array, "half", bit) for array in arrays])
        arrays = arrays + steps[-1]
        bit //= 2
    return arrays, steps


def per_device(voltages, scale_exps):
    volts = voltages[0]
    scale = jnp.exp2(scale_exps[0].astype(jnp.float32))
    blocks, _, count, inputs = volts.shape
    groups = lax.axis_size("freq")
    halves = lax.axis_size("half")
    half_in = inputs // 2
    odd = lax.axis_index("freq") % 2

    taps = jnp.broadcast_to(make_window(count).reshape(TAPS, count, 1), (TAPS, count, LANES))
    chunks = min(CHUNKS, count // groups)
    table = dft_table(count, groups, chunks)
    norm = 1.0 / (256.0 * math.sqrt(count))
    rim_start = blocks - (TAPS - 1)
    ahead = [(i, i + 2) for i in range(groups - 2)]

    def scaled(side, offset, width, first, ties):
        start = side * half_in + offset
        picked = lax.dynamic_slice(
            volts, (first, 0, 0, start), (blocks - first, 2, count, width)
        )
        factor = lax.dynamic_slice(scale, (first, start), (blocks - first, width))
        if ties:
            factor = after(factor, *ties)
        return (picked.astype(jnp.float32) * factor[:, None, None, :]).astype(jnp.bfloat16)

    piece_width = half_in // 4
    starts = [piece_width * k for k in range(4)]
    gives, got, edges, rims = [], [], [], []
    for k, start in enumerate(starts):
        ties = ([table, taps] if k == 1 else []) + got[k - 1 : k]
        gives.append(scaled(1 - odd, start, piece_width, 0, ties))
        got.append(flipped(gives[k], "freq", 1))
    for k, start in enumerate(starts):
        own = scaled(odd, start, piece_width, rim_start, rims[k - 1 : k])
        edges.append(jnp.where(odd == 1, own, got[k][rim_start:]))
        rims.append(lax.ppermute(edges[k], "freq", ahead))

    def transformed(first, last, split):
        return channelize(
            odd.reshape(1), volts, scale, got[first:last], rims[first:last], taps, table, groups,
            norm, starts[first], split,
        )

    def exchanged(array):
        return lax.all_to_all(array, "freq", split_axis=0, concat_axis=0, tiled=True)

    rows = inputs // halves
    half = lax.axis_index("half")
    row_start = jnp.stack([half * rows, half])
    weight = 1.0 / (halves * groups * blocks)
    per = count // groups // chunks

    first, second = [transformed(k, k + 1, 1)[0] for k in range(2)]
    turned = exchanged(after(first, got[2], rims[1], gives[3], edges[2]))
    gathered, steps = gather_steps(after(turned, second), [])
    early = [(starts[0], gathered)]
    turned = exchanged(after(second, got[3], rims[2], edges[3]))
    rims[3] = after(rims[3], *steps[0])
    last = transformed(2, 4, chunks)
    gathered, steps = gather_steps(after(turned, last[0]), [])
    early.append((starts[1], gathered))
    result, tokens = None, []
    for chunk, array in enumerate(last):
        turned = exchanged(array)
        if chunk == 0:
            turned = after(turned, *steps[0])
        elif chunk > 1 and chunk == chunks - 1:
            turned = after(turned, tokens[1])
        arrays, _ = gather_steps(turned, tokens[-1:])
        result, token = correlate(
            row_start, early + [(starts[2], arrays)], result, chunk, per, rows, count // groups,
            inputs, weight,
        )
        tokens.append(token)
    return result


def solution(mesh):
    return jax.shard_map(
        per_device,
        mesh=mesh,
        in_specs=(P("half", "freq", None, None, None), P("half", "freq", None)),
        out_specs=P("half", "freq", None, None),
        check_vma=False,
    )
```

```python
import functools
import math

import jax
import jax.numpy as jnp
from jax import lax
from jax.experimental import pallas as pl
from jax.experimental.pallas import tpu as pltpu
from jax.sharding import PartitionSpec as P

TAPS = 4
LANES = 128
VMEM = 56 * 1024 * 1024


def make_window(count):
    steps = jnp.arange(TAPS * count, dtype=jnp.float32) + 0.5
    return jnp.sinc(steps / count - 2.0) * (
        0.5 - 0.5 * jnp.cos(2.0 * math.pi * steps / (TAPS * count))
    )


def chunk_sizes(channels):
    return [channels // 8 * 3, channels // 4, channels // 4, channels // 8]


def dft_table(count, groups):
    index = jnp.arange(count, dtype=jnp.int32)
    first, channel = 0, jnp.zeros_like(index)
    for size in chunk_sizes(count // groups):
        inside = index - groups * first
        here = (inside >= 0) & (inside < groups * size)
        found = inside // size * (count // groups) + first + inside % size
        channel = jnp.where(here, found, channel)
        first += size
    angle = 2.0 * math.pi / count * (channel[:, None] * index[None, :] % count).astype(jnp.float32)
    cosine = jnp.cos(angle)
    sine = jnp.sin(angle)
    upper = jnp.concatenate([cosine, sine], axis=1)
    lower = jnp.concatenate([-sine, cosine], axis=1)
    return jnp.concatenate([upper, lower], axis=0).astype(jnp.bfloat16)


def channelize_kernel(norm, parts, odd_ref, own_ref, scale_ref, *rest):
    got_refs, rim_refs = rest[:parts], rest[parts : 2 * parts]
    taps_ref, table_ref = rest[2 * parts : 2 * parts + 2]
    outs, filtered, spread = rest[2 * parts + 2 : -2], rest[-2], rest[-1]
    blocks, _, count, width = own_ref.shape
    times = 2 * blocks
    together = filtered.shape[2] // width
    part_width = width // parts
    odd = odd_ref[0] == 1

    def filter_rows(step, carry):
        rows = pl.ds(pl.multiple_of(step * 16, 16), 16)
        weights = [taps_ref[q, rows, :] for q in range(TAPS)]
        for part in range(2):
            for lane in range(0, width, LANES):
                lanes = slice(lane, lane + LANES)
                got_ref, rim_ref = got_refs[lane // part_width], rim_refs[lane // part_width]
                inner = slice(lane % part_width, lane % part_width + LANES)
                own = [
                    own_ref[b, part, rows, lanes].astype(jnp.float32) * scale_ref[b : b + 1, lanes]
                    for b in range(blocks)
                ]
                got = [got_ref[b, part, rows, inner].astype(jnp.float32) for b in range(blocks)]
                line = [
                    rim_ref[b, part, rows, inner].astype(jnp.float32) for b in range(TAPS - 1)
                ]
                line += [jnp.where(odd, g, o) for g, o in zip(got, own)]
                line += [jnp.where(odd, o, g) for g, o in zip(got, own)]
                at = pl.ds(pl.multiple_of(part * count + step * 16, 16), 16)
                for t in range(times):
                    total = weights[0] * line[t]
                    for q in range(1, TAPS):
                        total = total + weights[q] * line[t + q]
                    place = t % together * width + lane
                    filtered[t // together, at, place : place + LANES] = total.astype(jnp.bfloat16)
        return carry

    lax.fori_loop(0, count // 16, filter_rows, 0)

    groups, _, depth, _ = outs[0].shape
    sizes = chunk_sizes(table_ref.shape[0] // (2 * groups))
    blocks_at, at, skip = [], 0, 0
    for chunk, size in enumerate(sizes):
        for group in range(groups):
            blocks_at.append((chunk, skip, group, size, at))
            at += size
        skip += size

    def some_times(step, carry):
        spectrum = (
            jnp.dot(table_ref[...], filtered[step], preferred_element_type=jnp.float32) * norm
        )
        for _, _, _, size, at in blocks_at:
            for part in range(2):
                first = part * count + at
                for place in range(0, together * width, LANES):
                    t = step * together + place // width
                    spread[
                        place % width // LANES,
                        pl.ds(at * depth + part * times + t, size, stride=depth),
                        :,
                    ] = spectrum[first : first + size, place : place + LANES]
        return carry

    lax.fori_loop(0, times // together, some_times, 0)

    for chunk, skip, group, size, at in blocks_at:
        out = outs[chunk] if len(outs) > 1 else outs[0]
        for c in range(size):
            base = (at + c) * depth
            place = c if len(outs) > 1 else skip + c
            for lane in range(width // LANES):
                out[group, place, :, lane * LANES : (lane + 1) * LANES] = spread[
                    lane, base : base + depth, :
                ].astype(jnp.bfloat16)


def channelize(odd, own, scale, got, rims, taps, table, groups, norm, offset, split):
    blocks, _, count, inputs = own.shape
    parts = len(got)
    part_width = got[0].shape[3]
    width = parts * part_width
    tiles = inputs // 2 // width
    skip = offset // width
    channels = count // groups
    depth = 4 * blocks
    together = max(1, 256 // width)
    out_shapes = [
        (groups, size, depth, width) for size in (chunk_sizes(channels) if split else [channels])
    ]
    grid_spec = pltpu.PrefetchScalarGridSpec(
        num_scalar_prefetch=1,
        grid=(1,),
        in_specs=[
            pl.BlockSpec((blocks, 2, count, width), lambda i, o: (0, 0, 0, o[0] * tiles + skip)),
            pl.BlockSpec((blocks, width), lambda i, o: (0, o[0] * tiles + skip)),
        ]
        + [pl.BlockSpec((blocks, 2, count, part_width), lambda i, o: (0, 0, 0, 0))] * parts
        + [pl.BlockSpec((TAPS - 1, 2, count, part_width), lambda i, o: (0, 0, 0, 0))] * parts
        + [
            pl.BlockSpec((TAPS, count, LANES), lambda i, o: (0, 0, 0)),
            pl.BlockSpec(table.shape, lambda i, o: (0, 0)),
        ],
        out_specs=[pl.BlockSpec(shape, lambda i, o: (0, 0, 0, 0)) for shape in out_shapes],
        scratch_shapes=[
            pltpu.VMEM((2 * blocks // together, 2 * count, together * width), jnp.bfloat16),
            pltpu.VMEM((width // LANES, count * depth, LANES), jnp.float32),
        ],
    )
    return pl.pallas_call(
        functools.partial(channelize_kernel, norm, parts),
        grid_spec=grid_spec,
        out_shape=[jax.ShapeDtypeStruct(shape, jnp.bfloat16) for shape in out_shapes],
        compiler_params=pltpu.CompilerParams(vmem_limit_bytes=VMEM),
        cost_estimate=pl.CostEstimate(
            flops=2 * (2 * blocks) * (2 * count) ** 2 * width,
            bytes_accessed=6 * blocks * count * width * 4,
            transcendentals=0,
        ),
    )(odd, own, scale, *got, *rims, taps, table)


def correlate_kernel(weight, layout, row_ref, *rest):
    out_ref, token_ref, mixed, columns = rest[-4:]
    token_ref[...] = jnp.zeros_like(token_ref)
    rows, channels, _, inputs = out_ref.shape
    half_in = inputs // 2
    deep = columns.shape[0]
    start = pl.multiple_of(row_ref[0], rows)
    me = row_ref[1]

    def one_channel(c, carry):
        at = 0
        for offset, masks, gathered in layout:
            for index, mask in enumerate(masks):
                piece = rest[at]
                if gathered:
                    piece = piece.at[me ^ mask]
                else:
                    at += 1
                pairs, sides, _, depth, width = piece.shape
                for side in range(sides):
                    first = side * half_in + offset
                    for pair in range(pairs):
                        base = (index * pairs + pair) * depth
                        columns[base : base + depth, first : first + width] = piece[pair, side, c]
            if gathered:
                at += 1
        left = columns[:, pl.ds(start, rows)].astype(jnp.float32) * weight
        parts = left.reshape(deep // depth, 2, depth // 2, rows)
        turned = jnp.stack([parts[:, 1], -parts[:, 0]], axis=1).reshape(deep, rows)
        for k in range(0, deep, LANES):
            mixed[k // LANES, pl.ds(0, rows, stride=2), :] = left[k : k + LANES].T
            mixed[k // LANES, pl.ds(1, rows, stride=2), :] = turned[k : k + LANES].T
        lhs = jnp.concatenate(
            [mixed[k].astype(jnp.bfloat16) for k in range(deep // LANES)], axis=1
        )
        product = jnp.dot(lhs, columns[...], preferred_element_type=jnp.float32)
        out_ref[:, c] = product.astype(jnp.bfloat16).reshape(rows, 2, inputs)
        return carry

    lax.fori_loop(0, channels, one_channel, 0)


def correlate(row_start, pieces, before, start, per, rows, count, inputs, weight):
    step = math.gcd(4, *chunk_sizes(count))
    in_specs, operands, layout = [], [row_start], []
    masks = segment_masks()
    for offset, arrays in pieces:
        gathered = not isinstance(arrays, list)
        for array in [arrays] if gathered else arrays:
            groups, channels, depth, width = array.shape[-4:]
            skip = start // step if channels > per else 0
            lead = array.shape[:-4]
            operands.append(array.reshape(*lead, groups // 2, 2, channels, depth, width))
            in_specs.append(
                pl.BlockSpec(
                    (*lead, groups // 2, 2, step, depth, width),
                    lambda i, r, skip=skip, zeros=(0,) * len(lead): (*zeros, 0, 0, skip + i, 0, 0),
                )
            )
        layout.append((offset, masks, gathered))
    deep = len(masks) * groups // 2 * depth
    aliases = {}
    if before is not None:
        in_specs.append(pl.BlockSpec(memory_space=pl.ANY))
        operands.append(before)
        aliases = {len(operands) - 1: 0}
    first = start // step
    return pl.pallas_call(
        functools.partial(correlate_kernel, weight, layout),
        grid_spec=pltpu.PrefetchScalarGridSpec(
            num_scalar_prefetch=1,
            grid=(per // step,),
            in_specs=in_specs,
            out_specs=[
                pl.BlockSpec((rows, step, 2, inputs), lambda i, r: (0, first + i, 0, 0)),
                pl.BlockSpec((8, LANES), lambda i, r: (0, 0)),
            ],
            scratch_shapes=[
                pltpu.VMEM((deep // LANES, 2 * rows, LANES), jnp.float32),
                pltpu.VMEM((deep, inputs), jnp.bfloat16),
            ],
        ),
        out_shape=[
            jax.ShapeDtypeStruct((rows, count, 2, inputs), jnp.bfloat16),
            jax.ShapeDtypeStruct((8, LANES), jnp.float32),
        ],
        input_output_aliases=aliases,
        compiler_params=pltpu.CompilerParams(vmem_limit_bytes=VMEM),
        cost_estimate=pl.CostEstimate(
            flops=2 * per * deep * 2 * rows * inputs,
            bytes_accessed=2 * (per * deep * inputs + rows * per * 2 * inputs),
            transcendentals=0,
        ),
    )(*operands)


def segment_masks():
    masks = [0]
    bit = lax.axis_size("half") // 2
    while bit:
        masks += [mask ^ bit for mask in masks]
        bit //= 2
    return masks


def after_kernel(*refs):
    del refs


def after(value, *others):
    whole = pl.BlockSpec(memory_space=pl.ANY)
    return pl.pallas_call(
        after_kernel,
        in_specs=[whole] * (1 + len(others)),
        out_specs=whole,
        out_shape=jax.ShapeDtypeStruct(value.shape, value.dtype),
        input_output_aliases={0: 0},
    )(value, *others)


def flipped(array, axis, bit):
    return lax.ppermute(array, axis, [(i, i ^ bit) for i in range(lax.axis_size(axis))])


def gather_steps(piece, ties):
    steps, arrays = [], [piece]
    bit = lax.axis_size("half") // 2
    while bit:
        if ties and steps:
            arrays = [after(array, *ties) for array in arrays]
        steps.append([flipped(array, "half", bit) for array in arrays])
        arrays = arrays + steps[-1]
        bit //= 2
    return arrays, steps


def per_device(voltages, scale_exps):
    volts = voltages[0]
    scale = jnp.exp2(scale_exps[0].astype(jnp.float32))
    blocks, _, count, inputs = volts.shape
    groups = lax.axis_size("freq")
    halves = lax.axis_size("half")
    half_in = inputs // 2
    odd = lax.axis_index("freq") % 2

    taps = jnp.broadcast_to(make_window(count).reshape(TAPS, count, 1), (TAPS, count, LANES))
    table = dft_table(count, groups)
    norm = 1.0 / (256.0 * math.sqrt(count))
    rim_start = blocks - (TAPS - 1)
    ahead = [(i, i + 2) for i in range(groups - 2)]

    def scaled(side, offset, width, first, ties):
        start = side * half_in + offset
        picked = lax.dynamic_slice(
            volts, (first, 0, 0, start), (blocks - first, 2, count, width)
        )
        factor = lax.dynamic_slice(scale, (first, start), (blocks - first, width))
        if ties:
            factor = after(factor, *ties)
        return (picked.astype(jnp.float32) * factor[:, None, None, :]).astype(jnp.bfloat16)

    piece_width = half_in // 4
    starts = [piece_width * k for k in range(4)]
    gives, got, edges, rims = [], [], [], []
    for k, start in enumerate(starts):
        ties = ([table, taps] if k == 1 else []) + got[k - 1 : k]
        gives.append(scaled(1 - odd, start, piece_width, 0, ties))
        got.append(flipped(gives[k], "freq", 1))
    for k, start in enumerate(starts):
        own = scaled(odd, start, piece_width, rim_start, rims[k - 1 : k])
        edges.append(jnp.where(odd == 1, own, got[k][rim_start:]))
        rims.append(lax.ppermute(edges[k], "freq", ahead))

    def transformed(first, last, split):
        return channelize(
            odd.reshape(1), volts, scale, got[first:last], rims[first:last], taps, table, groups,
            norm, starts[first], split,
        )

    def exchanged(array):
        return lax.all_to_all(array, "freq", split_axis=0, concat_axis=0, tiled=True)

    rows = inputs // halves
    half = lax.axis_index("half")
    row_start = jnp.stack([half * rows, half])
    weight = 1.0 / (halves * groups * blocks)
    first, second = [transformed(k, k + 1, False)[0] for k in range(2)]
    turned = exchanged(after(first, rims[3]))
    last = list(transformed(2, 4, True))
    gathered, steps = gather_steps(after(turned, last[0]), [])
    early = [(starts[0], gathered)]
    last[0] = after(last[0], *steps[0])
    gathered, steps = gather_steps(exchanged(second), [])
    early.append((starts[1], gathered))
    result, tokens, at = None, [], 0
    for chunk, array in enumerate(last):
        turned = exchanged(array)
        if chunk == 0:
            turned = after(turned, *steps[0])
        elif chunk == len(last) - 1:
            turned = after(turned, tokens[1])
        arrays, _ = gather_steps(turned, tokens[-1:])
        size = array.shape[1]
        result, token = correlate(
            row_start, early + [(starts[2], arrays)], result, at, size, rows, count // groups,
            inputs, weight,
        )
        tokens.append(token)
        at += size
    return result


def solution(mesh):
    return jax.shard_map(
        per_device,
        mesh=mesh,
        in_specs=(P("half", "freq", None, None, None), P("half", "freq", None)),
        out_specs=P("half", "freq", None, None),
        check_vma=False,
    )
```

```python
import functools
import math

import jax
import jax.numpy as jnp
from jax import lax
from jax.experimental import pallas as pl
from jax.experimental.pallas import tpu as pltpu
from jax.sharding import PartitionSpec as P

TAPS = 4
LANES = 128
VMEM = 56 * 1024 * 1024


def make_window(count):
    steps = jnp.arange(TAPS * count, dtype=jnp.float32) + 0.5
    return jnp.sinc(steps / count - 2.0) * (
        0.5 - 0.5 * jnp.cos(2.0 * math.pi * steps / (TAPS * count))
    )


def chunk_sizes(channels):
    return [channels // 8 * 3, channels // 4, channels // 4, channels // 8]


def dft_table(count, groups):
    index = jnp.arange(count, dtype=jnp.int32)
    first, channel = 0, jnp.zeros_like(index)
    for size in chunk_sizes(count // groups):
        inside = index - groups * first
        here = (inside >= 0) & (inside < groups * size)
        found = inside // size * (count // groups) + first + inside % size
        channel = jnp.where(here, found, channel)
        first += size
    angle = 2.0 * math.pi / count * (channel[:, None] * index[None, :] % count).astype(jnp.float32)
    cosine = jnp.cos(angle)
    sine = jnp.sin(angle)
    upper = jnp.concatenate([cosine, sine], axis=1)
    lower = jnp.concatenate([-sine, cosine], axis=1)
    return jnp.concatenate([upper, lower], axis=0).astype(jnp.bfloat16)


def channelize_kernel(norm, parts, odd_ref, own_ref, scale_ref, *rest):
    got_refs, rim_refs = rest[:parts], rest[parts : 2 * parts]
    taps_ref, table_ref = rest[2 * parts : 2 * parts + 2]
    outs, filtered, spread = rest[2 * parts + 2 : -2], rest[-2], rest[-1]
    blocks, _, count, width = own_ref.shape
    times = 2 * blocks
    together = filtered.shape[2] // width
    part_width = width // parts
    odd = odd_ref[0] == 1

    def filter_rows(step, carry):
        rows = pl.ds(pl.multiple_of(step * 16, 16), 16)
        weights = [taps_ref[q, rows, :] for q in range(TAPS)]
        for part in range(2):
            for lane in range(0, width, LANES):
                lanes = slice(lane, lane + LANES)
                got_ref, rim_ref = got_refs[lane // part_width], rim_refs[lane // part_width]
                inner = slice(lane % part_width, lane % part_width + LANES)
                own = [
                    own_ref[b, part, rows, lanes].astype(jnp.float32) * scale_ref[b : b + 1, lanes]
                    for b in range(blocks)
                ]
                got = [got_ref[b, part, rows, inner].astype(jnp.float32) for b in range(blocks)]
                line = [
                    rim_ref[b, part, rows, inner].astype(jnp.float32) for b in range(TAPS - 1)
                ]
                line += [jnp.where(odd, g, o) for g, o in zip(got, own)]
                line += [jnp.where(odd, o, g) for g, o in zip(got, own)]
                at = pl.ds(pl.multiple_of(part * count + step * 16, 16), 16)
                for t in range(times):
                    total = weights[0] * line[t]
                    for q in range(1, TAPS):
                        total = total + weights[q] * line[t + q]
                    place = t % together * width + lane
                    filtered[t // together, at, place : place + LANES] = total.astype(jnp.bfloat16)
        return carry

    lax.fori_loop(0, count // 16, filter_rows, 0)

    groups, _, depth, _ = outs[0].shape
    sizes = chunk_sizes(table_ref.shape[0] // (2 * groups))
    blocks_at, at, skip = [], 0, 0
    for chunk, size in enumerate(sizes):
        for group in range(groups):
            blocks_at.append((chunk, skip, group, size, at))
            at += size
        skip += size

    def some_times(step, carry):
        spectrum = (
            jnp.dot(table_ref[...], filtered[step], preferred_element_type=jnp.float32) * norm
        )
        for _, _, _, size, at in blocks_at:
            for part in range(2):
                first = part * count + at
                for place in range(0, together * width, LANES):
                    t = step * together + place // width
                    spread[
                        place % width // LANES,
                        pl.ds(at * depth + part * times + t, size, stride=depth),
                        :,
                    ] = spectrum[first : first + size, place : place + LANES]
        return carry

    lax.fori_loop(0, times // together, some_times, 0)

    for chunk, skip, group, size, at in blocks_at:
        out = outs[chunk] if len(outs) > 1 else outs[0]
        for c in range(size):
            base = (at + c) * depth
            place = c if len(outs) > 1 else skip + c
            for lane in range(width // LANES):
                out[group, place, :, lane * LANES : (lane + 1) * LANES] = spread[
                    lane, base : base + depth, :
                ].astype(jnp.bfloat16)


def channelize(odd, own, scale, got, rims, taps, table, groups, norm, offset, split):
    blocks, _, count, inputs = own.shape
    parts = len(got)
    part_width = got[0].shape[3]
    width = parts * part_width
    tiles = inputs // 2 // width
    skip = offset // width
    channels = count // groups
    depth = 4 * blocks
    together = max(1, 256 // width)
    out_shapes = [
        (groups, size, depth, width) for size in (chunk_sizes(channels) if split else [channels])
    ]
    grid_spec = pltpu.PrefetchScalarGridSpec(
        num_scalar_prefetch=1,
        grid=(1,),
        in_specs=[
            pl.BlockSpec((blocks, 2, count, width), lambda i, o: (0, 0, 0, o[0] * tiles + skip)),
            pl.BlockSpec((blocks, width), lambda i, o: (0, o[0] * tiles + skip)),
        ]
        + [pl.BlockSpec((blocks, 2, count, part_width), lambda i, o: (0, 0, 0, 0))] * parts
        + [pl.BlockSpec((TAPS - 1, 2, count, part_width), lambda i, o: (0, 0, 0, 0))] * parts
        + [
            pl.BlockSpec((TAPS, count, LANES), lambda i, o: (0, 0, 0)),
            pl.BlockSpec(table.shape, lambda i, o: (0, 0)),
        ],
        out_specs=[pl.BlockSpec(shape, lambda i, o: (0, 0, 0, 0)) for shape in out_shapes],
        scratch_shapes=[
            pltpu.VMEM((2 * blocks // together, 2 * count, together * width), jnp.bfloat16),
            pltpu.VMEM((width // LANES, count * depth, LANES), jnp.float32),
        ],
    )
    return pl.pallas_call(
        functools.partial(channelize_kernel, norm, parts),
        grid_spec=grid_spec,
        out_shape=[jax.ShapeDtypeStruct(shape, jnp.bfloat16) for shape in out_shapes],
        compiler_params=pltpu.CompilerParams(vmem_limit_bytes=VMEM),
        cost_estimate=pl.CostEstimate(
            flops=2 * (2 * blocks) * (2 * count) ** 2 * width,
            bytes_accessed=6 * blocks * count * width * 4,
            transcendentals=0,
        ),
    )(odd, own, scale, *got, *rims, taps, table)


def correlate_kernel(weight, layout, row_ref, *rest):
    out_ref, token_ref, mixed, columns = rest[-4:]
    token_ref[...] = jnp.zeros_like(token_ref)
    rows, channels, _, inputs = out_ref.shape
    half_in = inputs // 2
    deep = columns.shape[0]
    start = pl.multiple_of(row_ref[0], rows)
    me = row_ref[1]

    def one_channel(c, carry):
        at = 0
        for offset, masks, gathered in layout:
            for index, mask in enumerate(masks):
                piece = rest[at]
                if gathered:
                    piece = piece.at[me ^ mask]
                else:
                    at += 1
                pairs, sides, _, depth, width = piece.shape
                for side in range(sides):
                    first = side * half_in + offset
                    for pair in range(pairs):
                        base = (index * pairs + pair) * depth
                        columns[base : base + depth, first : first + width] = piece[pair, side, c]
            if gathered:
                at += 1
        left = columns[:, pl.ds(start, rows)].astype(jnp.float32) * weight
        parts = left.reshape(deep // depth, 2, depth // 2, rows)
        turned = jnp.stack([parts[:, 1], -parts[:, 0]], axis=1).reshape(deep, rows)
        for k in range(0, deep, LANES):
            mixed[k // LANES, pl.ds(0, rows, stride=2), :] = left[k : k + LANES].T
            mixed[k // LANES, pl.ds(1, rows, stride=2), :] = turned[k : k + LANES].T
        lhs = jnp.concatenate(
            [mixed[k].astype(jnp.bfloat16) for k in range(deep // LANES)], axis=1
        )
        product = jnp.dot(lhs, columns[...], preferred_element_type=jnp.float32)
        out_ref[:, c] = product.astype(jnp.bfloat16).reshape(rows, 2, inputs)
        return carry

    lax.fori_loop(0, channels, one_channel, 0)


def correlate(row_start, pieces, before, ties, start, per, rows, count, inputs, weight):
    step = math.gcd(4, *chunk_sizes(count))
    in_specs, operands, layout = [], [row_start], []
    masks = segment_masks()
    for offset, arrays in pieces:
        gathered = not isinstance(arrays, list)
        for array in [arrays] if gathered else arrays:
            groups, channels, depth, width = array.shape[-4:]
            skip = start // step if channels > per else 0
            lead = array.shape[:-4]
            operands.append(array.reshape(*lead, groups // 2, 2, channels, depth, width))
            in_specs.append(
                pl.BlockSpec(
                    (*lead, groups // 2, 2, step, depth, width),
                    lambda i, r, skip=skip, zeros=(0,) * len(lead): (*zeros, 0, 0, skip + i, 0, 0),
                )
            )
        layout.append((offset, masks, gathered))
    deep = len(masks) * groups // 2 * depth
    aliases = {}
    if before is not None:
        in_specs.append(pl.BlockSpec(memory_space=pl.ANY))
        operands.append(before)
        aliases = {len(operands) - 1: 0}
    in_specs += [pl.BlockSpec(memory_space=pl.ANY)] * len(ties)
    operands += ties
    first = start // step
    return pl.pallas_call(
        functools.partial(correlate_kernel, weight, layout),
        grid_spec=pltpu.PrefetchScalarGridSpec(
            num_scalar_prefetch=1,
            grid=(per // step,),
            in_specs=in_specs,
            out_specs=[
                pl.BlockSpec((rows, step, 2, inputs), lambda i, r: (0, first + i, 0, 0)),
                pl.BlockSpec((8, LANES), lambda i, r: (0, 0)),
            ],
            scratch_shapes=[
                pltpu.VMEM((deep // LANES, 2 * rows, LANES), jnp.float32),
                pltpu.VMEM((deep, inputs), jnp.bfloat16),
            ],
        ),
        out_shape=[
            jax.ShapeDtypeStruct((rows, count, 2, inputs), jnp.bfloat16),
            jax.ShapeDtypeStruct((8, LANES), jnp.float32),
        ],
        input_output_aliases=aliases,
        compiler_params=pltpu.CompilerParams(vmem_limit_bytes=VMEM),
        cost_estimate=pl.CostEstimate(
            flops=2 * per * deep * 2 * rows * inputs,
            bytes_accessed=2 * (per * deep * inputs + rows * per * 2 * inputs),
            transcendentals=0,
        ),
    )(*operands)


def segment_masks():
    masks = [0]
    bit = lax.axis_size("half") // 2
    while bit:
        masks += [mask ^ bit for mask in masks]
        bit //= 2
    return masks


def after_kernel(*refs):
    del refs


def after(value, *others):
    whole = pl.BlockSpec(memory_space=pl.ANY)
    return pl.pallas_call(
        after_kernel,
        in_specs=[whole] * (1 + len(others)),
        out_specs=whole,
        out_shape=jax.ShapeDtypeStruct(value.shape, value.dtype),
        input_output_aliases={0: 0},
    )(value, *others)


def flipped(array, axis, bit):
    return lax.ppermute(array, axis, [(i, i ^ bit) for i in range(lax.axis_size(axis))])


def gather_steps(piece, ties):
    steps, arrays = [], [piece]
    bit = lax.axis_size("half") // 2
    while bit:
        if ties and steps:
            arrays = [after(array, *ties) for array in arrays]
        steps.append([flipped(array, "half", bit) for array in arrays])
        arrays = arrays + steps[-1]
        bit //= 2
    return arrays, steps


def per_device(voltages, scale_exps):
    volts = voltages[0]
    scale = jnp.exp2(scale_exps[0].astype(jnp.float32))
    blocks, _, count, inputs = volts.shape
    groups = lax.axis_size("freq")
    halves = lax.axis_size("half")
    half_in = inputs // 2
    odd = lax.axis_index("freq") % 2

    taps = jnp.broadcast_to(make_window(count).reshape(TAPS, count, 1), (TAPS, count, LANES))
    table = dft_table(count, groups)
    norm = 1.0 / (256.0 * math.sqrt(count))
    rim_start = blocks - (TAPS - 1)
    ahead = [(i, i + 2) for i in range(groups - 2)]

    def scaled(side, offset, width, first, ties):
        start = side * half_in + offset
        picked = lax.dynamic_slice(
            volts, (first, 0, 0, start), (blocks - first, 2, count, width)
        )
        factor = lax.dynamic_slice(scale, (first, start), (blocks - first, width))
        if ties:
            factor = after(factor, *ties)
        return (picked.astype(jnp.float32) * factor[:, None, None, :]).astype(jnp.bfloat16)

    piece_width = half_in // 4
    starts = [piece_width * k for k in range(4)]
    gives, got, edges, rims = [], [], [], []
    for k, start in enumerate(starts):
        ties = ([table, taps] if k == 1 else []) + got[k - 1 : k]
        gives.append(scaled(1 - odd, start, piece_width, 0, ties))
        got.append(flipped(gives[k], "freq", 1))
    for k, start in enumerate(starts):
        own = scaled(odd, start, piece_width, rim_start, rims[k - 1 : k])
        edges.append(jnp.where(odd == 1, own, got[k][rim_start:]))
        rims.append(lax.ppermute(edges[k], "freq", ahead))

    def transformed(first, last, split):
        return channelize(
            odd.reshape(1), volts, scale, got[first:last], rims[first:last], taps, table, groups,
            norm, starts[first], split,
        )

    def exchanged(array):
        return lax.all_to_all(array, "freq", split_axis=0, concat_axis=0, tiled=True)

    rows = inputs // halves
    half = lax.axis_index("half")
    row_start = jnp.stack([half * rows, half])
    weight = 1.0 / (halves * groups * blocks)
    first, second = [transformed(k, k + 1, False)[0] for k in range(2)]
    turned = exchanged(after(first, rims[3]))
    last = list(transformed(2, 4, True))
    gathered, steps = gather_steps(after(turned, last[0]), [])
    early = [(starts[0], gathered)]
    second = exchanged(after(second, last[0]))
    last[0] = after(last[0], *steps[0])
    gathered, steps = gather_steps(second, [])
    early.append((starts[1], gathered))
    last = [exchanged(array) for array in last]
    result, tokens, at = None, [], 0
    for chunk, turned in enumerate(last):
        arrays, _ = gather_steps(turned, tokens[-1:])
        size = turned.shape[1]
        result, token = correlate(
            row_start, early + [(starts[2], arrays)], result, last[3:] if chunk == 1 else [], at,
            size, rows, count // groups, inputs, weight,
        )
        tokens.append(token)
        at += size
    return result


def solution(mesh):
    return jax.shard_map(
        per_device,
        mesh=mesh,
        in_specs=(P("half", "freq", None, None, None), P("half", "freq", None)),
        out_specs=P("half", "freq", None, None),
        check_vma=False,
    )
```

```python
import functools
import math

import jax
import jax.numpy as jnp
from jax import lax
from jax.experimental import pallas as pl
from jax.experimental.pallas import tpu as pltpu
from jax.sharding import PartitionSpec as P

TAPS = 4
LANES = 128
VMEM = 56 * 1024 * 1024


def make_window(count):
    steps = jnp.arange(TAPS * count, dtype=jnp.float32) + 0.5
    return jnp.sinc(steps / count - 2.0) * (
        0.5 - 0.5 * jnp.cos(2.0 * math.pi * steps / (TAPS * count))
    )


def chunk_sizes(channels):
    return [channels // 8 * 3, channels // 4, channels // 4, channels // 8]


def dft_table(count, groups):
    index = jnp.arange(count, dtype=jnp.int32)
    first, channel = 0, jnp.zeros_like(index)
    for size in chunk_sizes(count // groups):
        inside = index - groups * first
        here = (inside >= 0) & (inside < groups * size)
        found = inside // size * (count // groups) + first + inside % size
        channel = jnp.where(here, found, channel)
        first += size
    angle = 2.0 * math.pi / count * (channel[:, None] * index[None, :] % count).astype(jnp.float32)
    cosine = jnp.cos(angle)
    sine = jnp.sin(angle)
    upper = jnp.concatenate([cosine, sine], axis=1)
    lower = jnp.concatenate([-sine, cosine], axis=1)
    return jnp.concatenate([upper, lower], axis=0).astype(jnp.bfloat16)


def channelize_kernel(norm, parts, odd_ref, own_ref, scale_ref, *rest):
    got_refs, rim_refs = rest[:parts], rest[parts : 2 * parts]
    taps_ref, table_ref = rest[2 * parts : 2 * parts + 2]
    outs, filtered, spread = rest[2 * parts + 2 : -2], rest[-2], rest[-1]
    blocks, _, count, width = own_ref.shape
    times = 2 * blocks
    together = filtered.shape[2] // width
    part_width = width // parts
    odd = odd_ref[0] == 1

    def filter_rows(step, carry):
        rows = pl.ds(pl.multiple_of(step * 16, 16), 16)
        weights = [taps_ref[q, rows, :] for q in range(TAPS)]
        for part in range(2):
            for lane in range(0, width, LANES):
                lanes = slice(lane, lane + LANES)
                got_ref, rim_ref = got_refs[lane // part_width], rim_refs[lane // part_width]
                inner = slice(lane % part_width, lane % part_width + LANES)
                own = [
                    own_ref[b, part, rows, lanes].astype(jnp.float32) * scale_ref[b : b + 1, lanes]
                    for b in range(blocks)
                ]
                got = [got_ref[b, part, rows, inner].astype(jnp.float32) for b in range(blocks)]
                line = [
                    rim_ref[b, part, rows, inner].astype(jnp.float32) for b in range(TAPS - 1)
                ]
                line += [jnp.where(odd, g, o) for g, o in zip(got, own)]
                line += [jnp.where(odd, o, g) for g, o in zip(got, own)]
                at = pl.ds(pl.multiple_of(part * count + step * 16, 16), 16)
                for t in range(times):
                    total = weights[0] * line[t]
                    for q in range(1, TAPS):
                        total = total + weights[q] * line[t + q]
                    place = t % together * width + lane
                    filtered[t // together, at, place : place + LANES] = total.astype(jnp.bfloat16)
        return carry

    lax.fori_loop(0, count // 16, filter_rows, 0)

    groups, _, depth, _ = outs[0].shape
    sizes = chunk_sizes(table_ref.shape[0] // (2 * groups))
    blocks_at, at, skip = [], 0, 0
    for chunk, size in enumerate(sizes):
        for group in range(groups):
            blocks_at.append((chunk, skip, group, size, at))
            at += size
        skip += size

    def some_times(step, carry):
        spectrum = (
            jnp.dot(table_ref[...], filtered[step], preferred_element_type=jnp.float32) * norm
        )
        for _, _, _, size, at in blocks_at:
            for part in range(2):
                first = part * count + at
                for place in range(0, together * width, LANES):
                    t = step * together + place // width
                    spread[
                        place % width // LANES,
                        pl.ds(at * depth + part * times + t, size, stride=depth),
                        :,
                    ] = spectrum[first : first + size, place : place + LANES]
        return carry

    lax.fori_loop(0, times // together, some_times, 0)

    for chunk, skip, group, size, at in blocks_at:
        out = outs[chunk] if len(outs) > 1 else outs[0]
        for c in range(size):
            base = (at + c) * depth
            place = c if len(outs) > 1 else skip + c
            for lane in range(width // LANES):
                out[group, place, :, lane * LANES : (lane + 1) * LANES] = spread[
                    lane, base : base + depth, :
                ].astype(jnp.bfloat16)


def channelize(odd, own, scale, got, rims, taps, table, groups, norm, offset, split):
    blocks, _, count, inputs = own.shape
    parts = len(got)
    part_width = got[0].shape[3]
    width = parts * part_width
    tiles = inputs // 2 // width
    skip = offset // width
    channels = count // groups
    depth = 4 * blocks
    together = max(1, 256 // width)
    out_shapes = [
        (groups, size, depth, width) for size in (chunk_sizes(channels) if split else [channels])
    ]
    grid_spec = pltpu.PrefetchScalarGridSpec(
        num_scalar_prefetch=1,
        grid=(1,),
        in_specs=[
            pl.BlockSpec((blocks, 2, count, width), lambda i, o: (0, 0, 0, o[0] * tiles + skip)),
            pl.BlockSpec((blocks, width), lambda i, o: (0, o[0] * tiles + skip)),
        ]
        + [pl.BlockSpec((blocks, 2, count, part_width), lambda i, o: (0, 0, 0, 0))] * parts
        + [pl.BlockSpec((TAPS - 1, 2, count, part_width), lambda i, o: (0, 0, 0, 0))] * parts
        + [
            pl.BlockSpec((TAPS, count, LANES), lambda i, o: (0, 0, 0)),
            pl.BlockSpec(table.shape, lambda i, o: (0, 0)),
        ],
        out_specs=[pl.BlockSpec(shape, lambda i, o: (0, 0, 0, 0)) for shape in out_shapes],
        scratch_shapes=[
            pltpu.VMEM((2 * blocks // together, 2 * count, together * width), jnp.bfloat16),
            pltpu.VMEM((width // LANES, count * depth, LANES), jnp.float32),
        ],
    )
    return pl.pallas_call(
        functools.partial(channelize_kernel, norm, parts),
        grid_spec=grid_spec,
        out_shape=[jax.ShapeDtypeStruct(shape, jnp.bfloat16) for shape in out_shapes],
        compiler_params=pltpu.CompilerParams(vmem_limit_bytes=VMEM),
        cost_estimate=pl.CostEstimate(
            flops=2 * (2 * blocks) * (2 * count) ** 2 * width,
            bytes_accessed=6 * blocks * count * width * 4,
            transcendentals=0,
        ),
    )(odd, own, scale, *got, *rims, taps, table)


def correlate_kernel(weight, layout, row_ref, *rest):
    out_ref, token_ref, mixed, columns = rest[-4:]
    token_ref[...] = jnp.zeros_like(token_ref)
    rows, channels, _, inputs = out_ref.shape
    half_in = inputs // 2
    deep = columns.shape[0]
    start = pl.multiple_of(row_ref[0], rows)
    me = row_ref[1]

    def one_channel(c, carry):
        at = 0
        for offset, masks, gathered in layout:
            for index, mask in enumerate(masks):
                piece = rest[at]
                if gathered:
                    piece = piece.at[me ^ mask]
                else:
                    at += 1
                pairs, sides, _, depth, width = piece.shape
                for side in range(sides):
                    first = side * half_in + offset
                    for pair in range(pairs):
                        base = (index * pairs + pair) * (depth // 2)
                        for part in range(2):
                            to = part * (deep // 2) + base
                            columns[to : to + depth // 2, first : first + width] = piece[
                                pair, side, c, part * (depth // 2) : (part + 1) * (depth // 2)
                            ]
            if gathered:
                at += 1
        left = columns[:, pl.ds(start, rows)].astype(jnp.float32) * weight
        for k in range(0, deep // 2, LANES):
            real = left[k : k + LANES].T
            imaginary = left[deep // 2 + k : deep // 2 + k + LANES].T
            near, far = k // LANES, (deep // 2 + k) // LANES
            mixed[near, pl.ds(0, rows, stride=2), :] = real
            mixed[near, pl.ds(1, rows, stride=2), :] = imaginary
            mixed[far, pl.ds(0, rows, stride=2), :] = imaginary
            mixed[far, pl.ds(1, rows, stride=2), :] = -real
        lhs = jnp.concatenate(
            [mixed[k].astype(jnp.bfloat16) for k in range(deep // LANES)], axis=1
        )
        product = jnp.dot(lhs, columns[...], preferred_element_type=jnp.float32)
        out_ref[:, c] = product.astype(jnp.bfloat16).reshape(rows, 2, inputs)
        return carry

    lax.fori_loop(0, channels, one_channel, 0)


def correlate(row_start, pieces, before, ties, start, per, rows, count, inputs, weight):
    step = math.gcd(4, *chunk_sizes(count))
    in_specs, operands, layout = [], [row_start], []
    masks = segment_masks()
    for offset, arrays in pieces:
        gathered = not isinstance(arrays, list)
        for array in [arrays] if gathered else arrays:
            groups, channels, depth, width = array.shape[-4:]
            skip = start // step if channels > per else 0
            lead = array.shape[:-4]
            operands.append(array.reshape(*lead, groups // 2, 2, channels, depth, width))
            in_specs.append(
                pl.BlockSpec(
                    (*lead, groups // 2, 2, step, depth, width),
                    lambda i, r, skip=skip, zeros=(0,) * len(lead): (*zeros, 0, 0, skip + i, 0, 0),
                )
            )
        layout.append((offset, masks, gathered))
    deep = len(masks) * groups // 2 * depth
    aliases = {}
    if before is not None:
        in_specs.append(pl.BlockSpec(memory_space=pl.ANY))
        operands.append(before)
        aliases = {len(operands) - 1: 0}
    in_specs += [pl.BlockSpec(memory_space=pl.ANY)] * len(ties)
    operands += ties
    first = start // step
    return pl.pallas_call(
        functools.partial(correlate_kernel, weight, layout),
        grid_spec=pltpu.PrefetchScalarGridSpec(
            num_scalar_prefetch=1,
            grid=(per // step,),
            in_specs=in_specs,
            out_specs=[
                pl.BlockSpec((rows, step, 2, inputs), lambda i, r: (0, first + i, 0, 0)),
                pl.BlockSpec((8, LANES), lambda i, r: (0, 0)),
            ],
            scratch_shapes=[
                pltpu.VMEM((deep // LANES, 2 * rows, LANES), jnp.float32),
                pltpu.VMEM((deep, inputs), jnp.bfloat16),
            ],
        ),
        out_shape=[
            jax.ShapeDtypeStruct((rows, count, 2, inputs), jnp.bfloat16),
            jax.ShapeDtypeStruct((8, LANES), jnp.float32),
        ],
        input_output_aliases=aliases,
        compiler_params=pltpu.CompilerParams(vmem_limit_bytes=VMEM),
        cost_estimate=pl.CostEstimate(
            flops=2 * per * deep * 2 * rows * inputs,
            bytes_accessed=2 * (per * deep * inputs + rows * per * 2 * inputs),
            transcendentals=0,
        ),
    )(*operands)


def segment_masks():
    masks = [0]
    bit = lax.axis_size("half") // 2
    while bit:
        masks += [mask ^ bit for mask in masks]
        bit //= 2
    return masks


def after_kernel(*refs):
    del refs


def after(value, *others):
    whole = pl.BlockSpec(memory_space=pl.ANY)
    return pl.pallas_call(
        after_kernel,
        in_specs=[whole] * (1 + len(others)),
        out_specs=whole,
        out_shape=jax.ShapeDtypeStruct(value.shape, value.dtype),
        input_output_aliases={0: 0},
    )(value, *others)


def flipped(array, axis, bit):
    return lax.ppermute(array, axis, [(i, i ^ bit) for i in range(lax.axis_size(axis))])


def gather_steps(piece, ties, begun=()):
    steps, arrays = [], [piece]
    bit = lax.axis_size("half") // 2
    while bit:
        if ties and steps:
            arrays = [after(array, *ties) for array in arrays]
        if begun and not steps:
            steps.append(list(begun))
        else:
            steps.append([flipped(array, "half", bit) for array in arrays])
        arrays = arrays + steps[-1]
        bit //= 2
    return arrays, steps


def per_device(voltages, scale_exps):
    volts = voltages[0]
    scale = jnp.exp2(scale_exps[0].astype(jnp.float32))
    blocks, _, count, inputs = volts.shape
    groups = lax.axis_size("freq")
    halves = lax.axis_size("half")
    half_in = inputs // 2
    odd = lax.axis_index("freq") % 2

    taps = jnp.broadcast_to(make_window(count).reshape(TAPS, count, 1), (TAPS, count, LANES))
    table = dft_table(count, groups)
    norm = 1.0 / (256.0 * math.sqrt(count))
    rim_start = blocks - (TAPS - 1)
    ahead = [(i, i + 2) for i in range(groups - 2)]

    def scaled(side, offset, width, first, ties):
        start = side * half_in + offset
        picked = lax.dynamic_slice(
            volts, (first, 0, 0, start), (blocks - first, 2, count, width)
        )
        factor = lax.dynamic_slice(scale, (first, start), (blocks - first, width))
        if ties:
            factor = after(factor, *ties)
        return (picked.astype(jnp.float32) * factor[:, None, None, :]).astype(jnp.bfloat16)

    piece_width = half_in // 4
    starts = [piece_width * k for k in range(4)]
    gives, got, edges, rims = [], [], [], []
    for k, start in enumerate(starts):
        ties = ([table, taps] if k == 1 else []) + got[k - 1 : k]
        gives.append(scaled(1 - odd, start, piece_width, 0, ties))
        got.append(flipped(gives[k], "freq", 1))
    for k, start in enumerate(starts):
        own = scaled(odd, start, piece_width, rim_start, rims[k - 1 : k])
        edges.append(jnp.where(odd == 1, own, got[k][rim_start:]))
        rims.append(lax.ppermute(edges[k], "freq", ahead))

    def transformed(first, last, split):
        return channelize(
            odd.reshape(1), volts, scale, got[first:last], rims[first:last], taps, table, groups,
            norm, starts[first], split,
        )

    def exchanged(array):
        return lax.all_to_all(array, "freq", split_axis=0, concat_axis=0, tiled=True)

    rows = inputs // halves
    half = lax.axis_index("half")
    row_start = jnp.stack([half * rows, half])
    weight = 1.0 / (halves * groups * blocks)
    first, second = [transformed(k, k + 1, False)[0] for k in range(2)]
    turned = exchanged(after(first, rims[3]))
    last = list(transformed(2, 4, True))
    gathered, steps = gather_steps(after(turned, last[0]), [])
    early = [(starts[0], gathered)]
    second = exchanged(after(second, last[0]))
    last[0] = after(last[0], *steps[0])
    gathered, steps = gather_steps(second, [])
    early.append((starts[1], gathered))
    last = [exchanged(array) for array in last]
    result, tokens, at = None, [], 0
    gathers = [flipped(last[3], "half", halves // 2)]
    for chunk, turned in enumerate(last):
        ties = [[], last[3:], gathers, []][chunk]
        arrays, _ = gather_steps(
            turned, tokens[-1:] if chunk < 3 else [], gathers if chunk == 3 else []
        )
        size = turned.shape[1]
        result, token = correlate(
            row_start, early + [(starts[2], arrays)], result, ties, at, size, rows,
            count // groups, inputs, weight,
        )
        tokens.append(token)
        at += size
    return result


def solution(mesh):
    return jax.shard_map(
        per_device,
        mesh=mesh,
        in_specs=(P("half", "freq", None, None, None), P("half", "freq", None)),
        out_specs=P("half", "freq", None, None),
        check_vma=False,
    )
```
